32 devices in a mesh: dp: 16 (over z, y, core), blk: 2 (over x).
Axes of the slice: x: 2, y: 2, z: 4, core: 2. Of those that a mesh axis runs over, the one named last changes fastest.
Arguments:
- queries: bfloat16 [2, 64, 32, 128], P('blk', 'dp'), may hold values from -6 to 6
- passages: bfloat16 [2, 256, 192, 128], P('blk', 'dp'), may hold values from -6 to 6
- passage_lengths: int32 [2, 256], P('blk', 'dp'), may hold values from 32 to 192
- positives: bfloat16 [2, 64, 192, 128], P('blk', 'dp'), may hold values from -6 to 6
- positive_lengths: int32 [2, 64], P('blk', 'dp'), may hold values from 32 to 192
- owners: int32 [2, 64, 32, 1], P('blk', 'dp'), may hold values from 0 to 15; in each aligned block of 128 rows (0 to 127, 128 to 255, ..., all dimensions but the last counted through in order) at most 16 rows name the same one
- local_ids: int32 [2, 64, 32], P('blk', 'dp'), may hold values from 0 to 15
- teacher: float32 [2, 64, 32], P('blk', 'dp'), may hold values from -12 to 12
Outputs:
- student: float32 [2, 64, 32], P('blk', 'dp')
- distill: float32 [2, 64], P('blk', 'dp')
- contrast: float32 [2, 64], P('blk', 'dp')
The draws below stay inside these ranges and needn't reach their ends.
Inputs may be any that keep to these rules, and one draw needn't show every extreme that they name: `owners`: among the 128 candidate pairs of the queries of one device, no owner is named more than 16 times, a bound that some block reaches.
All inputs are finite; a program needn't handle non-finite values.
Results may differ from the reference program's by a relative error of at most 0.00062.
Values may be sent and summed in bfloat16 or wider, within the bound.
No kernel may reach another device: no remote copies, remote signals or barrier semaphores. Data moves between devices by JAX's collectives and lax.ppermute only.
A program may use at most 64 MiB of HBM per device.

```python
import math
import jax
import jax.numpy as jnp
import numpy as np
from jax import lax

D = 128
QLEN = 32
LMAX = 192
CAND = 32
Q_DEV = 4
PASS_DEV = 16
CAP = 16
QUERIES_G = 64
PASSAGES_G = 256
N_DP = 16
N_BLK = 2


def plant(result, stream_key, low, top_value):
    longest = result.shape.index(max(result.shape))
    spots = []
    for shift in (0, 1):
        where = [jax.random.randint(jax.random.fold_in(stream_key, axis), (), 0, length) for axis, length in enumerate(result.shape)]
        where[longest] = (where[longest] + shift) % result.shape[longest]
        spots.append(tuple(where))
    return result.at[spots[0]].set(low).at[spots[1]].set(top_value)


def steps_of(stream_key, dims, shards, least, high):
    def one(position, parts):
        heights = jax.random.uniform(jax.random.fold_in(jax.random.fold_in(stream_key, 6), position), (parts,), jnp.float32, least / len(shards), high / len(shards))
        return jnp.repeat(jnp.exp(heights), dims[position] // parts).reshape((-1,) + (1,) * (len(dims) - position - 1))

    gain = one(*shards[0])
    for cut in shards[1:]:
        gain = gain * one(*cut)
    return gain


def shared_out(own_key, own, number, rows, count, top, reach, skew):
    order = jax.random.permutation(own_key, count)
    crowded, ordinary = shares(count, rows * top, reach, skew, True), shares(count, rows * top, reach, skew, False)
    places = jnp.arange(count)

    def named(sizes, rotation):
        used = int((sizes > 0).sum())
        fixed = max(1, used // 4)
        passed = fixed + (places - fixed + rotation * (used - fixed)) % max(1, count - fixed)
        return jnp.zeros((count,), jnp.int32).at[order[jnp.where(places < fixed, places, passed)]].set(jnp.asarray(sizes, jnp.int32))

    sizes = jnp.where(number % 4 == 0, named(crowded, number // 4), named(ordinary, number - number // 4 - 1))
    mixed = jax.random.permutation(jax.random.fold_in(own, 3), count)
    giver, sink = mixed[0:count // 2 * 2:2], mixed[1:count // 2 * 2:2]
    room = jnp.minimum(sizes[giver] - 1, reach - sizes[sink]) // 2
    room = jnp.where((giver == order[0]) | (sink == order[0]) | (sizes[sink] == 0), 0, jnp.maximum(room, 0))
    passed = jax.random.randint(jax.random.fold_in(own, 4), (count // 2,), 0, 1 << 20) % (room + 1)
    sizes = sizes.at[giver].add(-passed).at[sink].add(passed)
    items = jnp.searchsorted(jnp.cumsum(sizes), jnp.arange(rows * top), side="right").astype(jnp.int32)
    listing = items.reshape(top, rows).T
    listing = listing[jax.random.permutation(jax.random.fold_in(own, 1), rows)]
    rotation = jax.random.randint(jax.random.fold_in(own, 2), (rows, 1), 0, top)
    return jnp.take_along_axis(listing, (jnp.arange(top)[None, :] + rotation) % top, axis=1)


def shares(count, total, limit, lean, full):
    weights = [(1 << 20) // math.isqrt(rank ** lean) + 1 for rank in range(1, count + 1)]
    largest = limit if full else min(limit, max(-(-total // count), total * weights[0] // sum(weights)))
    least = 1 if total - largest >= count - 1 else 0
    given, spare = [largest] + [least] * (count - 1), total - largest - least * (count - 1)
    while spare > 0:
        free = [i for i in range(1, count) if given[i] < largest] or [i for i in range(1, count) if given[i] < limit]
        whole, budget = sum([weights[i] for i in free]), spare
        for i in free:
            extra = min(limit - given[i], max(1, budget * weights[i] // whole), spare)
            given[i] = given[i] + extra
            spare = spare - extra
    return np.array(given)


def centred(key, extent, deviation, limit, shards=(), held_as=jnp.bfloat16):
    factor_of = steps_of(key, extent, shards, -0.22, 0.18) if shards else 1.0
    values = jax.random.normal(key, extent, jnp.float32) * deviation * factor_of
    return jnp.minimum(jnp.maximum(values, -limit), limit).astype(held_as)


def setup_inputs(seed: int = 0) -> dict:
    arg_keys = jax.random.split(jax.random.key(seed), 9)
    queries = centred(arg_keys[0], (N_BLK, QUERIES_G, QLEN, D), 1.0, 6.0, ((0, 2), (1, 16)))
    passages = centred(arg_keys[1], (N_BLK, PASSAGES_G, LMAX, D), 1.0, 6.0, ((0, 2), (1, 16)))
    passage_lengths = plant(jax.random.randint(arg_keys[2], (N_BLK, PASSAGES_G), LMAX // 6, LMAX + 1), jax.random.fold_in(arg_keys[2], 1), LMAX // 6, LMAX).astype(jnp.int32)
    positives = centred(arg_keys[3], (N_BLK, QUERIES_G, LMAX, D), 1.0, 6.0, ((0, 2), (1, 16)))
    positive_lengths = plant(jax.random.randint(arg_keys[4], (N_BLK, QUERIES_G), LMAX // 6, LMAX + 1), jax.random.fold_in(arg_keys[4], 1), LMAX // 6, LMAX).astype(jnp.int32)
    owners_keys = jax.random.split(jax.random.fold_in(arg_keys[5], 1), N_BLK * QUERIES_G * CAND // (Q_DEV * CAND))
    owners_turns = jax.random.permutation(jax.random.fold_in(arg_keys[5], 3), N_BLK * QUERIES_G * CAND // (Q_DEV * CAND))
    owners = jax.vmap(lambda own, number: shared_out(jax.random.fold_in(arg_keys[5], 2), own, number, Q_DEV * CAND, N_DP, 1, CAP, 2))(owners_keys, owners_turns).reshape((N_BLK, QUERIES_G, CAND, 1))
    local_ids = plant(jax.random.randint(arg_keys[6], (N_BLK, QUERIES_G, CAND), 0, PASS_DEV), jax.random.fold_in(arg_keys[6], 1), 0, PASS_DEV - 1).astype(jnp.int32)
    teacher = centred(arg_keys[7], (N_BLK, QUERIES_G, CAND), 2.0, 12.0, ((0, 2), (1, 16)), jnp.float32)
    return {"queries": queries, "passages": passages, "passage_lengths": passage_lengths, "positives": positives, "positive_lengths": positive_lengths, "owners": owners, "local_ids": local_ids, "teacher": teacher}


def unit_rows(values):
    wide = values.astype(jnp.float32)
    total = lax.optimization_barrier(jnp.sum(wide * wide, axis=-1, keepdims=True)) + 1e-06
    return (wide * lax.rsqrt(total)).astype(jnp.bfloat16)

def late_score(query, document_rows, lengths):
    similarity_matrix = jnp.einsum('qd,kld->kql', query.astype(jnp.float32), document_rows.astype(jnp.float32))
    usable = jnp.arange(document_rows.shape[1]).astype(jnp.int32)[None, None, :] < lengths[:, None, None]
    similarity_matrix = jnp.where(usable, similarity_matrix, -1000000000.0)
    return lax.optimization_barrier(jnp.sum(lax.optimization_barrier(jnp.max(similarity_matrix, axis=2)), axis=1))

def reference(queries, passages, passage_lengths, positives, positive_lengths, owners, local_ids, teacher):
    query_unit = unit_rows(queries)
    passage_unit = unit_rows(passages)
    positive_unit = unit_rows(positives)
    flat_ids = (owners[..., 0] * PASS_DEV + local_ids).astype(jnp.int32)

    def per_group(group):
        group_queries, group_passages, group_lengths, group_ids = group

        def per_query(inner):
            query, selected_entries = inner
            return late_score(query, group_passages[selected_entries], group_lengths[selected_entries])
        return lax.map(per_query, (group_queries, group_ids))
    student = lax.map(per_group, (query_unit, passage_unit, passage_lengths, flat_ids))
    log_teacher = teacher - jnp.log(lax.optimization_barrier(jnp.sum(jnp.exp(teacher), axis=-1, keepdims=True)))
    log_student = student - jnp.log(lax.optimization_barrier(jnp.sum(jnp.exp(student), axis=-1, keepdims=True)))
    distill = lax.optimization_barrier(jnp.sum(jnp.exp(log_teacher) * (log_teacher - log_student), axis=-1))
    split_queries = jnp.moveaxis(query_unit.reshape(N_BLK, N_DP, Q_DEV, QLEN, D), 1, 0)
    split_docs = jnp.moveaxis(positive_unit.reshape(N_BLK, N_DP, Q_DEV, LMAX, D), 1, 0)
    split_lengths = jnp.moveaxis(positive_lengths.reshape(N_BLK, N_DP, Q_DEV), 1, 0)

    def per_column(column):
        column_queries, column_docs, column_lengths = column
        document_rows = column_docs.reshape(N_BLK * Q_DEV, LMAX, D)
        lengths = column_lengths.reshape(N_BLK * Q_DEV)

        def per_query(query):
            return late_score(query, document_rows, lengths)
        return lax.map(per_query, column_queries.reshape(N_BLK * Q_DEV, QLEN, D))
    logits = lax.map(per_column, (split_queries, split_docs, split_lengths))
    logits = jnp.moveaxis(logits.reshape(N_DP, N_BLK, Q_DEV, N_BLK * Q_DEV), 0, 1)
    logits = logits.reshape(N_BLK, N_DP * Q_DEV, N_BLK * Q_DEV)
    group_index = jnp.arange(N_BLK).astype(jnp.int32)[:, None]
    query_index = (jnp.arange(N_DP * Q_DEV) % Q_DEV).astype(jnp.int32)[None, :]
    own_column = (group_index * Q_DEV + query_index).astype(jnp.int32)
    own_logit = jnp.take_along_axis(logits, own_column[:, :, None], axis=2)[..., 0]
    contrast = jnp.log(lax.optimization_barrier(jnp.sum(jnp.exp(logits), axis=-1))) - own_logit
    return (student, distill, contrast)
```

```python
import functools

import jax
import jax.numpy as jnp
from jax import lax
from jax.experimental import pallas as pl
from jax.experimental.pallas import tpu as pltpu
from jax.sharding import PartitionSpec as P

VMEM = pl.BlockSpec(memory_space=pltpu.VMEM)
SMEM = pl.BlockSpec(memory_space=pltpu.SMEM)
LIMIT = 32 * 1024 * 1024


def unit(values):
    wide = values.astype(jnp.float32)
    total = jnp.sum(wide * wide, axis=-1, keepdims=True) + 1e-06
    return (wide * lax.rsqrt(total)).astype(jnp.bfloat16)


def kept_unit(rows, kept):
    place = lax.broadcasted_iota(jnp.int32, (rows.shape[0], 1), 0)
    wide = rows.astype(jnp.float32)
    return unit(jnp.where(place < kept, wide, wide[0:1]))


def group_sum(values, width):
    lanes = values.shape[1]
    row = lax.broadcasted_iota(jnp.int32, (lanes, lanes), 0) // width
    column = lax.broadcasted_iota(jnp.int32, (lanes, lanes), 1) // width
    same = (row == column).astype(jnp.bfloat16)
    high = values.astype(jnp.bfloat16)
    rest = values - high.astype(jnp.float32)
    middle = rest.astype(jnp.bfloat16)
    low = (rest - middle.astype(jnp.float32)).astype(jnp.bfloat16)
    parts = [jnp.dot(part, same, preferred_element_type=jnp.float32) for part in (high, middle, low)]
    return parts[0] + (parts[1] + parts[2])


def best_match(tokens, query_rows):
    similar = lax.dot_general(
        tokens, query_rows, (((1,), (1,)), ((), ())), preferred_element_type=jnp.float32
    )
    return jnp.max(similar, axis=0, keepdims=True)


def prepare_kernel(kept_ref, rows_ref, out_ref):
    def one(i, carry):
        out_ref[i] = kept_unit(rows_ref[i], kept_ref[0, i])
        return carry

    lax.fori_loop(0, rows_ref.shape[0], one, 0, unroll=4)


def prepare(rows, kept):
    return pl.pallas_call(
        prepare_kernel,
        out_shape=jax.ShapeDtypeStruct(rows.shape, rows.dtype),
        in_specs=[SMEM, VMEM],
        out_specs=VMEM,
        compiler_params=pltpu.CompilerParams(vmem_limit_bytes=LIMIT),
        cost_estimate=pl.CostEstimate(flops=16 * rows.size, bytes_accessed=4 * rows.size, transcendentals=0),
    )(kept, rows)


def score_kernel(qlen, count, *refs):
    query_refs, (near_ref, far_ref, out_ref, best_ref) = refs[:count], refs[count:]
    near = near_ref.shape[0]
    total = near + far_ref.shape[0]
    lanes = query_refs[0].shape[1]
    row = lax.broadcasted_iota(jnp.int32, (total, lanes), 0)
    column = lax.broadcasted_iota(jnp.int32, (total, lanes), 1) % qlen
    start = 0
    queries = [ref[i] for ref in query_refs for i in range(ref.shape[0])]
    while start < len(queries):
        block = [unit(q) for q in queries[start : start + 2]]
        joined = jnp.concatenate(block, axis=0)
        width = joined.shape[0]
        for i in range(total):
            tokens = near_ref[i] if i < near else far_ref[i - near]
            best_ref[i : i + 1, :width] = best_match(tokens, joined)
        for s in range(len(block)):
            summed = group_sum(best_ref[:, s * lanes : (s + 1) * lanes], qlen)
            out_ref[start + s : start + s + 1, :] = jnp.sum(
                jnp.where(row == column, summed, 0.0), axis=0, keepdims=True
            )
        start += 2


def score(query_list, near, far, qlen):
    lanes = query_list[0].shape[1]
    sources = sum(q.shape[0] for q in query_list)
    total = near.shape[0] + far.shape[0]
    return pl.pallas_call(
        functools.partial(score_kernel, qlen, len(query_list)),
        out_shape=jax.ShapeDtypeStruct((sources, lanes), jnp.float32),
        in_specs=[VMEM] * (len(query_list) + 2),
        out_specs=VMEM,
        scratch_shapes=[pltpu.VMEM((total, 2 * lanes), jnp.float32)],
        compiler_params=pltpu.CompilerParams(vmem_limit_bytes=LIMIT),
        cost_estimate=pl.CostEstimate(
            flops=2 * sources * lanes * near.shape[2] * total * near.shape[1],
            bytes_accessed=2 * (near.size + far.size),
            transcendentals=0,
        ),
    )(*query_list, near, far)


def contrast_kernel(qlen, query_ref, own_ref, other_ref, out_ref, best_ref):
    queries = unit(query_ref[...])
    lanes = queries.shape[0]
    docs = own_ref.shape[0]
    total = docs + other_ref.shape[0]
    for i in range(total):
        tokens = own_ref[i] if i < docs else other_ref[i - docs]
        best_ref[i : i + 1, :] = best_match(tokens, queries)
    logits = group_sum(best_ref[...], qlen)
    row = lax.broadcasted_iota(jnp.int32, (total, lanes), 0)
    query = lax.broadcasted_iota(jnp.int32, (total, lanes), 1) // qlen
    own = jnp.sum(jnp.where(row == query, logits, 0.0), axis=0, keepdims=True)
    loss = jnp.log(jnp.sum(jnp.exp(logits), axis=0, keepdims=True)) - own
    place = (lax.broadcasted_iota(jnp.int32, (8, lanes), 1) * qlen) % lanes
    spread = jnp.take_along_axis(jnp.broadcast_to(loss, (8, lanes)), place, axis=1)
    out_ref[...] = spread[0:1, : lanes // qlen]


def contrast_loss(query_rows, own, other, qlen):
    lanes = query_rows.shape[0]
    total = own.shape[0] + other.shape[0]
    return pl.pallas_call(
        functools.partial(contrast_kernel, qlen),
        out_shape=jax.ShapeDtypeStruct((1, lanes // qlen), jnp.float32),
        in_specs=[VMEM, VMEM, VMEM],
        out_specs=VMEM,
        scratch_shapes=[pltpu.VMEM((total, lanes), jnp.float32)],
        compiler_params=pltpu.CompilerParams(vmem_limit_bytes=LIMIT),
        cost_estimate=pl.CostEstimate(
            flops=2 * lanes * own.shape[2] * total * own.shape[1], bytes_accessed=4 * own.size, transcendentals=0
        ),
    )(query_rows, own, other)


def flat_lanes(rows, pad_ref, lanes):
    queries, width = rows.shape
    pad_ref[:queries, :width] = rows
    place = lax.broadcasted_iota(jnp.int32, (8, lanes), 1)
    spread = jnp.take_along_axis(pad_ref[...], place % width, axis=1)
    row = lax.broadcasted_iota(jnp.int32, (8, lanes), 0)
    return jnp.sum(jnp.where(row == place // width, spread, 0), axis=0, keepdims=True)


def distill_kernel(returned_ref, where_ref, lane_ref, teacher_ref, student_ref, distill_ref, pad_ref, ints_ref):
    queries, width = teacher_ref.shape[1:]
    scorers, lanes = returned_ref.shape
    teacher = flat_lanes(teacher_ref[0], pad_ref, lanes)
    whose = flat_lanes(where_ref[...], ints_ref, lanes)
    lane = flat_lanes(lane_ref[...], ints_ref, lanes)
    lane = lane + lax.broadcasted_iota(jnp.int32, (1, lanes), 1) // width * (lanes // queries)
    returned = returned_ref[...]
    picked = jnp.take_along_axis(returned, jnp.broadcast_to(lane, (scorers, lanes)), axis=1)
    row = lax.broadcasted_iota(jnp.int32, (scorers, lanes), 0)
    student = jnp.sum(jnp.where(row == whose, picked, 0.0), axis=0, keepdims=True)
    log_teacher = teacher - jnp.log(group_sum(jnp.exp(teacher), width))
    log_student = student - jnp.log(group_sum(jnp.exp(student), width))
    loss = group_sum(jnp.exp(log_teacher) * (log_teacher - log_student), width)
    first = lax.broadcasted_iota(jnp.int32, (8, lanes), 0)
    place = lax.broadcasted_iota(jnp.int32, (8, lanes), 1)
    spread = jnp.take_along_axis(jnp.broadcast_to(student, (8, lanes)), (first * width + place) % lanes, axis=1)
    student_ref[0] = spread[:queries, :width]
    spread = jnp.take_along_axis(jnp.broadcast_to(loss, (8, lanes)), (place * width) % lanes, axis=1)
    distill_ref[...] = spread[0:1, :queries]


def distill_loss(returned, whose, lane, teacher):
    lanes = returned.shape[1]
    return pl.pallas_call(
        distill_kernel,
        out_shape=(
            jax.ShapeDtypeStruct(teacher.shape, jnp.float32),
            jax.ShapeDtypeStruct(teacher.shape[:2], jnp.float32),
        ),
        in_specs=[VMEM] * 4,
        out_specs=(VMEM, VMEM),
        scratch_shapes=[pltpu.VMEM((8, lanes), jnp.float32), pltpu.VMEM((8, lanes), jnp.int32)],
        compiler_params=pltpu.CompilerParams(vmem_limit_bytes=LIMIT),
    )(returned, whose, lane, teacher)


def swap(values, axis, bit):
    return lax.ppermute(values, axis, [(i, i ^ bit) for i in range(lax.axis_size(axis))])


def per_device(
    queries, passages, passage_lengths, positives, positive_lengths, owners, local_ids, teacher
):
    peers = lax.axis_size("dp")
    groups = lax.axis_size("blk")
    me = lax.axis_index("dp")
    query_count, qlen = queries.shape[1:3]
    pass_count = passages.shape[1]
    own_rows = queries.reshape(1, query_count * qlen, queries.shape[3])
    bits = [1 << n for n in range(1, peers.bit_length() - 1)]

    first = swap(own_rows, "dp", bits[-1])
    near = prepare(passages[0], passage_lengths)
    far = swap(near, "dp", 1)
    own_docs = prepare(positives[0], positive_lengths)
    other_docs = jnp.concatenate(
        [
            lax.ppermute(own_docs, "blk", [(i, (i + k) % groups) for i in range(groups)])
            for k in range(1, groups)
        ],
        axis=0,
    )

    held = jnp.concatenate([own_rows, first], axis=0)
    scored = [score([own_rows, first], near, far, qlen)]
    for bit in reversed(bits[:-1]):
        got = swap(held, "dp", bit)
        scored.append(score([got], near, far, qlen))
        held = jnp.concatenate([held, got], axis=0)
    contrast = contrast_loss(own_rows[0], own_docs, other_docs, qlen)

    back = jnp.concatenate(scored, axis=0)[None]
    for bit in bits:
        half = back.shape[1] // 2
        back = jnp.concatenate([back[:, :half], swap(back[:, half:], "dp", bit)], axis=0)
    returned = back.reshape(peers // 2, query_count * qlen)

    apart = owners[0, :, :, 0] ^ me
    student, distill = distill_loss(returned, apart >> 1, (apart & 1) * pass_count + local_ids[0], teacher)
    return (student, distill, contrast)


def solution(mesh):
    in_specs = (
        P("blk", "dp", None, None),
        P("blk", "dp", None, None),
        P("blk", "dp"),
        P("blk", "dp", None, None),
        P("blk", "dp"),
        P("blk", "dp", None, None),
        P("blk", "dp", None),
        P("blk", "dp", None),
    )
    out_specs = (P("blk", "dp", None), P("blk", "dp"), P("blk", "dp"))
    return jax.shard_map(
        per_device, mesh=mesh, in_specs=in_specs, out_specs=out_specs, check_vma=False
    )
```

```python
import functools

import jax
import jax.numpy as jnp
from jax import lax
from jax.experimental import pallas as pl
from jax.experimental.pallas import tpu as pltpu
from jax.sharding import PartitionSpec as P

VMEM = pl.BlockSpec(memory_space=pltpu.VMEM)
SMEM = pl.BlockSpec(memory_space=pltpu.SMEM)
LIMIT = 32 * 1024 * 1024


def unit(values):
    wide = values.astype(jnp.float32)
    total = jnp.sum(wide * wide, axis=-1, keepdims=True) + 1e-06
    return (wide * lax.rsqrt(total)).astype(jnp.bfloat16)


def kept_unit(rows, kept):
    place = lax.broadcasted_iota(jnp.int32, (rows.shape[0], 1), 0)
    wide = rows.astype(jnp.float32)
    return unit(jnp.where(place < kept, wide, wide[0:1]))


def group_sum(values, width):
    lanes = values.shape[1]
    row = lax.broadcasted_iota(jnp.int32, (lanes, lanes), 0) // width
    column = lax.broadcasted_iota(jnp.int32, (lanes, lanes), 1) // width
    same = (row == column).astype(jnp.bfloat16)
    high = values.astype(jnp.bfloat16)
    rest = values - high.astype(jnp.float32)
    middle = rest.astype(jnp.bfloat16)
    low = (rest - middle.astype(jnp.float32)).astype(jnp.bfloat16)
    parts = [jnp.dot(part, same, preferred_element_type=jnp.float32) for part in (high, middle, low)]
    return parts[0] + (parts[1] + parts[2])


def best_match(tokens, query_rows):
    similar = lax.dot_general(
        tokens, query_rows, (((1,), (1,)), ((), ())), preferred_element_type=jnp.float32
    )
    return jnp.max(similar, axis=0, keepdims=True)


def prepare_kernel(kept_ref, rows_ref, out_ref):
    def one(i, carry):
        out_ref[i] = kept_unit(rows_ref[i], kept_ref[0, i])
        return carry

    lax.fori_loop(0, rows_ref.shape[0], one, 0, unroll=4)


def prepare(rows, kept):
    return pl.pallas_call(
        prepare_kernel,
        out_shape=jax.ShapeDtypeStruct(rows.shape, rows.dtype),
        in_specs=[SMEM, VMEM],
        out_specs=VMEM,
        compiler_params=pltpu.CompilerParams(vmem_limit_bytes=LIMIT),
        cost_estimate=pl.CostEstimate(flops=16 * rows.size, bytes_accessed=4 * rows.size, transcendentals=0),
    )(kept, rows)


def score_kernel(qlen, count, *refs):
    query_refs, (near_ref, far_ref, out_ref, best_ref) = refs[:count], refs[count:]
    near = near_ref.shape[0]
    total = near + far_ref.shape[0]
    lanes = query_refs[0].shape[1]
    row = lax.broadcasted_iota(jnp.int32, (total, lanes), 0)
    column = lax.broadcasted_iota(jnp.int32, (total, lanes), 1) % qlen
    start = 0
    queries = [ref[i] for ref in query_refs for i in range(ref.shape[0])]
    while start < len(queries):
        block = [unit(q) for q in queries[start : start + 2]]
        joined = jnp.concatenate(block, axis=0)
        width = joined.shape[0]
        for i in range(total):
            tokens = near_ref[i] if i < near else far_ref[i - near]
            best_ref[i : i + 1, :width] = best_match(tokens, joined)
        for s in range(len(block)):
            summed = group_sum(best_ref[:, s * lanes : (s + 1) * lanes], qlen)
            out_ref[start + s : start + s + 1, :] = jnp.sum(
                jnp.where(row == column, summed, 0.0), axis=0, keepdims=True
            )
        start += 2


def score(query_list, near, far, qlen):
    lanes = query_list[0].shape[1]
    sources = sum(q.shape[0] for q in query_list)
    total = near.shape[0] + far.shape[0]
    return pl.pallas_call(
        functools.partial(score_kernel, qlen, len(query_list)),
        out_shape=jax.ShapeDtypeStruct((sources, lanes), jnp.float32),
        in_specs=[VMEM] * (len(query_list) + 2),
        out_specs=VMEM,
        scratch_shapes=[pltpu.VMEM((total, 2 * lanes), jnp.float32)],
        compiler_params=pltpu.CompilerParams(vmem_limit_bytes=LIMIT),
        cost_estimate=pl.CostEstimate(
            flops=2 * sources * lanes * near.shape[2] * total * near.shape[1],
            bytes_accessed=2 * (near.size + far.size),
            transcendentals=0,
        ),
    )(*query_list, near, far)


def flat_lanes(rows, pad_ref, lanes):
    queries, width = rows.shape
    pad_ref[:queries, :width] = rows
    place = lax.broadcasted_iota(jnp.int32, (8, lanes), 1)
    spread = jnp.take_along_axis(pad_ref[...], place % width, axis=1)
    row = lax.broadcasted_iota(jnp.int32, (8, lanes), 0)
    return jnp.sum(jnp.where(row == place // width, spread, 0), axis=0, keepdims=True)


def early_kernel(
    qlen, query_ref, own_ref, other_ref, where_ref, lane_ref, teacher_ref,
    contrast_ref, teach_ref, index_ref, best_ref, pad_ref, ints_ref,
):
    queries = unit(query_ref[...])
    lanes = queries.shape[0]
    docs = own_ref.shape[0]
    total = docs + other_ref.shape[0]
    for i in range(total):
        tokens = own_ref[i] if i < docs else other_ref[i - docs]
        best_ref[i : i + 1, :] = best_match(tokens, queries)
    logits = group_sum(best_ref[...], qlen)
    row = lax.broadcasted_iota(jnp.int32, (total, lanes), 0)
    query = lax.broadcasted_iota(jnp.int32, (total, lanes), 1) // qlen
    own = jnp.sum(jnp.where(row == query, logits, 0.0), axis=0, keepdims=True)
    loss = jnp.log(jnp.sum(jnp.exp(logits), axis=0, keepdims=True)) - own
    place = (lax.broadcasted_iota(jnp.int32, (8, lanes), 1) * qlen) % lanes
    spread = jnp.take_along_axis(jnp.broadcast_to(loss, (8, lanes)), place, axis=1)
    contrast_ref[...] = spread[0:1, : lanes // qlen]

    count, width = teacher_ref.shape[1:]
    teacher = flat_lanes(teacher_ref[0], pad_ref, lanes)
    log_teacher = teacher - jnp.log(group_sum(jnp.exp(teacher), width))
    teach_ref[0:1, :] = log_teacher
    teach_ref[1:2, :] = jnp.exp(log_teacher)
    index_ref[0:1, :] = flat_lanes(where_ref[...], ints_ref, lanes)
    lane = flat_lanes(lane_ref[...], ints_ref, lanes)
    index_ref[1:2, :] = lane + lax.broadcasted_iota(jnp.int32, (1, lanes), 1) // width * (lanes // count)


def early(query_rows, own, other, whose, lane, teacher, qlen):
    lanes = query_rows.shape[0]
    total = own.shape[0] + other.shape[0]
    return pl.pallas_call(
        functools.partial(early_kernel, qlen),
        out_shape=(
            jax.ShapeDtypeStruct(teacher.shape[:2], jnp.float32),
            jax.ShapeDtypeStruct((2, lanes), jnp.float32),
            jax.ShapeDtypeStruct((2, lanes), jnp.int32),
        ),
        in_specs=[VMEM] * 6,
        out_specs=(VMEM, VMEM, VMEM),
        scratch_shapes=[
            pltpu.VMEM((total, lanes), jnp.float32),
            pltpu.VMEM((8, lanes), jnp.float32),
            pltpu.VMEM((8, lanes), jnp.int32),
        ],
        compiler_params=pltpu.CompilerParams(vmem_limit_bytes=LIMIT),
        cost_estimate=pl.CostEstimate(
            flops=2 * lanes * own.shape[2] * total * own.shape[1], bytes_accessed=4 * own.size, transcendentals=0
        ),
    )(query_rows, own, other, whose, lane, teacher)


def distill_kernel(returned_ref, teach_ref, index_ref, student_ref, distill_ref):
    queries, width = student_ref.shape[1:]
    scorers, lanes = returned_ref.shape
    picked = jnp.take_along_axis(
        returned_ref[...], jnp.broadcast_to(index_ref[1:2, :], (scorers, lanes)), axis=1
    )
    row = lax.broadcasted_iota(jnp.int32, (scorers, lanes), 0)
    student = jnp.sum(jnp.where(row == index_ref[0:1, :], picked, 0.0), axis=0, keepdims=True)
    first = lax.broadcasted_iota(jnp.int32, (8, lanes), 0)
    place = lax.broadcasted_iota(jnp.int32, (8, lanes), 1)
    spread = jnp.take_along_axis(jnp.broadcast_to(student, (8, lanes)), (first * width + place) % lanes, axis=1)
    student_ref[0] = spread[:queries, :width]
    log_student = student - jnp.log(group_sum(jnp.exp(student), width))
    loss = group_sum(teach_ref[1:2, :] * (teach_ref[0:1, :] - log_student), width)
    spread = jnp.take_along_axis(jnp.broadcast_to(loss, (8, lanes)), (place * width) % lanes, axis=1)
    distill_ref[...] = spread[0:1, :queries]


def distill_loss(returned, teach, index, shape):
    return pl.pallas_call(
        distill_kernel,
        out_shape=(
            jax.ShapeDtypeStruct(shape, jnp.float32),
            jax.ShapeDtypeStruct(shape[:2], jnp.float32),
        ),
        in_specs=[VMEM] * 3,
        out_specs=(VMEM, VMEM),
        compiler_params=pltpu.CompilerParams(vmem_limit_bytes=LIMIT),
    )(returned, teach, index)


def swap(values, axis, bit):
    return lax.ppermute(values, axis, [(i, i ^ bit) for i in range(lax.axis_size(axis))])


def per_device(
    queries, passages, passage_lengths, positives, positive_lengths, owners, local_ids, teacher
):
    peers = lax.axis_size("dp")
    groups = lax.axis_size("blk")
    me = lax.axis_index("dp")
    query_count, qlen = queries.shape[1:3]
    pass_count = passages.shape[1]
    own_rows = queries.reshape(1, query_count * qlen, queries.shape[3])
    bits = [(1 << n) | 1 for n in range(1, peers.bit_length() - 1)]

    tie = lax.optimization_barrier

    last = bits[0]
    held = fresh = own_rows
    crossed = []
    parts = []
    near = prepare(passages[0], passage_lengths)
    for n, bit in enumerate(reversed(bits[1:])):
        got = swap(held, "dp", bit)
        crossed.append(swap(fresh, "dp", last))
        if n == 0:
            near, got = tie((near, got))
            far = swap(near, "dp", 1)
            parts.append(score([own_rows, got], near, far, qlen))
        else:
            got, parts[-1] = tie((got, parts[-1]))
            parts.append(score([got], near, far, qlen))
        held, fresh = jnp.concatenate([held, got], axis=0), got
    rest = score(crossed, near, far, qlen)
    final = swap(fresh, "dp", last)
    final, rest, parts[-1] = tie((final, rest, parts[-1]))
    final = score([final], near, far, qlen)

    final, positives, owners, local_ids = tie((final, positives, owners, local_ids))
    own_docs = prepare(positives[0], positive_lengths)
    other_docs = jnp.concatenate(
        [
            lax.ppermute(own_docs, "blk", [(i, (i + k) % groups) for i in range(groups)])
            for k in range(1, groups)
        ],
        axis=0,
    )
    apart = owners[0, :, :, 0] ^ me
    odd = functools.reduce(lambda x, n: x ^ (apart >> n), range(1, peers.bit_length() - 1), apart) & 1
    lane = odd * pass_count + local_ids[0]
    contrast, teach, index = early(own_rows[0], own_docs, other_docs, apart >> 1, lane, teacher, qlen)

    back = jnp.concatenate(parts + [rest, final], axis=0)[None]
    for n, bit in enumerate(bits):
        half = back.shape[1] // 2
        arrived = swap(back[:, half:], "dp", bit)
        if n == 0:
            arrived, own_docs = tie((arrived, own_docs))
        if n == len(bits) - 1:
            arrived, teach = tie((arrived, teach))
        back = jnp.concatenate([back[:, :half], arrived], axis=0)
    returned = back.reshape(peers // 2, query_count * qlen)
    student, distill = distill_loss(returned, teach, index, teacher.shape)
    return (student, distill, contrast)


def solution(mesh):
    in_specs = (
        P("blk", "dp", None, None),
        P("blk", "dp", None, None),
        P("blk", "dp"),
        P("blk", "dp", None, None),
        P("blk", "dp"),
        P("blk", "dp", None, None),
        P("blk", "dp", None),
        P("blk", "dp", None),
    )
    out_specs = (P("blk", "dp", None), P("blk", "dp"), P("blk", "dp"))
    return jax.shard_map(
        per_device, mesh=mesh, in_specs=in_specs, out_specs=out_specs, check_vma=False
    )
```

```python
import functools

import jax
import jax.numpy as jnp
from jax import lax
from jax.experimental import pallas as pl
from jax.experimental.pallas import tpu as pltpu
from jax.sharding import PartitionSpec as P

VMEM = pl.BlockSpec(memory_space=pltpu.VMEM)
SMEM = pl.BlockSpec(memory_space=pltpu.SMEM)
LIMIT = 32 * 1024 * 1024


def unit(values):
    wide = values.astype(jnp.float32)
    total = jnp.sum(wide * wide, axis=-1, keepdims=True) + 1e-06
    return (wide * lax.rsqrt(total)).astype(jnp.bfloat16)


def kept_unit(rows, kept):
    place = lax.broadcasted_iota(jnp.int32, (rows.shape[0], 1), 0)
    wide = rows.astype(jnp.float32)
    return unit(jnp.where(place < kept, wide, wide[0:1]))


def group_sum(values, width):
    lanes = values.shape[1]
    row = lax.broadcasted_iota(jnp.int32, (lanes, lanes), 0) // width
    column = lax.broadcasted_iota(jnp.int32, (lanes, lanes), 1) // width
    same = (row == column).astype(jnp.bfloat16)
    high = values.astype(jnp.bfloat16)
    rest = values - high.astype(jnp.float32)
    middle = rest.astype(jnp.bfloat16)
    low = (rest - middle.astype(jnp.float32)).astype(jnp.bfloat16)
    stacked = jnp.concatenate([high, middle, low], axis=0)
    sums = jnp.dot(stacked, same, preferred_element_type=jnp.float32)
    count = values.shape[0]
    return sums[:count] + (sums[count : 2 * count] + sums[2 * count :])


def best_match(tokens, query_rows):
    similar = lax.dot_general(
        tokens, query_rows, (((1,), (1,)), ((), ())), preferred_element_type=jnp.float32
    )
    return jnp.max(similar, axis=0, keepdims=True)


def prepare_kernel(kept_ref, rows_ref, out_ref):
    def one(i, carry):
        out_ref[i] = kept_unit(rows_ref[i], kept_ref[0, i])
        return carry

    lax.fori_loop(0, rows_ref.shape[0], one, 0, unroll=4)


def prepare(rows, kept):
    return pl.pallas_call(
        prepare_kernel,
        out_shape=jax.ShapeDtypeStruct(rows.shape, rows.dtype),
        in_specs=[SMEM, VMEM],
        out_specs=VMEM,
        compiler_params=pltpu.CompilerParams(vmem_limit_bytes=LIMIT),
        cost_estimate=pl.CostEstimate(flops=16 * rows.size, bytes_accessed=4 * rows.size, transcendentals=0),
    )(kept, rows)


def score_kernel(qlen, count, *refs):
    query_refs, (near_ref, far_ref, out_ref, best_ref) = refs[:count], refs[count:]
    near = near_ref.shape[0]
    total = near + far_ref.shape[0]
    lanes = query_refs[0].shape[1]
    row = lax.broadcasted_iota(jnp.int32, (total, lanes), 0)
    column = lax.broadcasted_iota(jnp.int32, (total, lanes), 1) % qlen
    start = 0
    queries = [ref[i] for ref in query_refs for i in range(ref.shape[0])]
    while start < len(queries):
        block = [unit(q) for q in queries[start : start + 2]]
        joined = jnp.concatenate(block, axis=0)
        width = joined.shape[0]
        for i in range(total):
            tokens = near_ref[i] if i < near else far_ref[i - near]
            best_ref[i : i + 1, :width] = best_match(tokens, joined)
        for s in range(len(block)):
            summed = group_sum(best_ref[:, s * lanes : (s + 1) * lanes], qlen)
            out_ref[start + s : start + s + 1, :] = jnp.sum(
                jnp.where(row == column, summed, 0.0), axis=0, keepdims=True
            )
        start += 2


def score(query_list, near, far, qlen):
    lanes = query_list[0].shape[1]
    sources = sum(q.shape[0] for q in query_list)
    total = near.shape[0] + far.shape[0]
    return pl.pallas_call(
        functools.partial(score_kernel, qlen, len(query_list)),
        out_shape=jax.ShapeDtypeStruct((sources, lanes), jnp.float32),
        in_specs=[VMEM] * (len(query_list) + 2),
        out_specs=VMEM,
        scratch_shapes=[pltpu.VMEM((total, 2 * lanes), jnp.float32)],
        compiler_params=pltpu.CompilerParams(vmem_limit_bytes=LIMIT),
        cost_estimate=pl.CostEstimate(
            flops=2 * sources * lanes * near.shape[2] * total * near.shape[1],
            bytes_accessed=2 * (near.size + far.size),
            transcendentals=0,
        ),
    )(*query_list, near, far)


def flat_lanes(rows, pad_ref, lanes):
    queries, width = rows.shape
    pad_ref[:queries, :width] = rows
    place = lax.broadcasted_iota(jnp.int32, (8, lanes), 1)
    spread = jnp.take_along_axis(pad_ref[...], place % width, axis=1)
    row = lax.broadcasted_iota(jnp.int32, (8, lanes), 0)
    return jnp.sum(jnp.where(row == place // width, spread, 0), axis=0, keepdims=True)


def contrast_kernel(qlen, query_ref, own_ref, other_ref, contrast_ref, best_ref):
    queries = unit(query_ref[...])
    lanes = queries.shape[0]
    docs = own_ref.shape[0]
    total = docs + other_ref.shape[0]
    for i in range(total):
        tokens = own_ref[i] if i < docs else other_ref[i - docs]
        best_ref[i : i + 1, :] = best_match(tokens, queries)
    logits = group_sum(best_ref[...], qlen)
    row = lax.broadcasted_iota(jnp.int32, (total, lanes), 0)
    query = lax.broadcasted_iota(jnp.int32, (total, lanes), 1) // qlen
    own = jnp.sum(jnp.where(row == query, logits, 0.0), axis=0, keepdims=True)
    loss = jnp.log(jnp.sum(jnp.exp(logits), axis=0, keepdims=True)) - own
    place = (lax.broadcasted_iota(jnp.int32, (8, lanes), 1) * qlen) % lanes
    spread = jnp.take_along_axis(jnp.broadcast_to(loss, (8, lanes)), place, axis=1)
    contrast_ref[...] = spread[0:1, : lanes // qlen]


def contrast_loss(query_rows, own, other, qlen):
    lanes = query_rows.shape[0]
    total = own.shape[0] + other.shape[0]
    return pl.pallas_call(
        functools.partial(contrast_kernel, qlen),
        out_shape=jax.ShapeDtypeStruct((1, lanes // qlen), jnp.float32),
        in_specs=[VMEM] * 3,
        out_specs=VMEM,
        scratch_shapes=[pltpu.VMEM((total, lanes), jnp.float32)],
        compiler_params=pltpu.CompilerParams(vmem_limit_bytes=LIMIT),
        cost_estimate=pl.CostEstimate(
            flops=2 * lanes * own.shape[2] * total * own.shape[1], bytes_accessed=4 * own.size, transcendentals=0
        ),
    )(query_rows, own, other)


def teach_kernel(where_ref, lane_ref, teacher_ref, teach_ref, index_ref, pad_ref, ints_ref):
    count, width = teacher_ref.shape[1:]
    lanes = teach_ref.shape[1]
    teacher = flat_lanes(teacher_ref[0], pad_ref, lanes)
    log_teacher = teacher - jnp.log(group_sum(jnp.exp(teacher), width))
    teach_ref[0:1, :] = log_teacher
    teach_ref[1:2, :] = jnp.exp(log_teacher)
    index_ref[0:1, :] = flat_lanes(where_ref[...], ints_ref, lanes)
    lane = flat_lanes(lane_ref[...], ints_ref, lanes)
    index_ref[1:2, :] = lane + lax.broadcasted_iota(jnp.int32, (1, lanes), 1) // width * (lanes // count)


def teach_rows(whose, lane, teacher, lanes):
    return pl.pallas_call(
        teach_kernel,
        out_shape=(
            jax.ShapeDtypeStruct((2, lanes), jnp.float32),
            jax.ShapeDtypeStruct((2, lanes), jnp.int32),
        ),
        in_specs=[VMEM] * 3,
        out_specs=(VMEM, VMEM),
        scratch_shapes=[pltpu.VMEM((8, lanes), jnp.float32), pltpu.VMEM((8, lanes), jnp.int32)],
        compiler_params=pltpu.CompilerParams(vmem_limit_bytes=LIMIT),
    )(whose, lane, teacher)


def distill_kernel(returned_ref, teach_ref, index_ref, student_ref, distill_ref):
    queries, width = student_ref.shape[1:]
    scorers, lanes = returned_ref.shape
    picked = jnp.take_along_axis(
        returned_ref[...], jnp.broadcast_to(index_ref[1:2, :], (scorers, lanes)), axis=1
    )
    row = lax.broadcasted_iota(jnp.int32, (scorers, lanes), 0)
    student = jnp.sum(jnp.where(row == index_ref[0:1, :], picked, 0.0), axis=0, keepdims=True)
    first = lax.broadcasted_iota(jnp.int32, (8, lanes), 0)
    place = lax.broadcasted_iota(jnp.int32, (8, lanes), 1)
    spread = jnp.take_along_axis(jnp.broadcast_to(student, (8, lanes)), (first * width + place) % lanes, axis=1)
    student_ref[0] = spread[:queries, :width]
    log_student = student - jnp.log(group_sum(jnp.exp(student), width))
    loss = group_sum(teach_ref[1:2, :] * (teach_ref[0:1, :] - log_student), width)
    spread = jnp.take_along_axis(jnp.broadcast_to(loss, (8, lanes)), (place * width) % lanes, axis=1)
    distill_ref[...] = spread[0:1, :queries]


def distill_loss(returned, teach, index, shape):
    return pl.pallas_call(
        distill_kernel,
        out_shape=(
            jax.ShapeDtypeStruct(shape, jnp.float32),
            jax.ShapeDtypeStruct(shape[:2], jnp.float32),
        ),
        in_specs=[VMEM] * 3,
        out_specs=(VMEM, VMEM),
        compiler_params=pltpu.CompilerParams(vmem_limit_bytes=LIMIT),
    )(returned, teach, index)


def swap(values, axis, bit):
    return lax.ppermute(values, axis, [(i, i ^ bit) for i in range(lax.axis_size(axis))])


def per_device(
    queries, passages, passage_lengths, positives, positive_lengths, owners, local_ids, teacher
):
    peers = lax.axis_size("dp")
    groups = lax.axis_size("blk")
    me = lax.axis_index("dp")
    query_count, qlen = queries.shape[1:3]
    pass_count = passages.shape[1]
    own_rows = queries.reshape(1, query_count * qlen, queries.shape[3])
    bits = [(1 << n) | 1 for n in range(1, peers.bit_length() - 1)]

    tie = lax.optimization_barrier

    last = bits[0]
    near = prepare(passages[0], passage_lengths)
    got = swap(own_rows, "dp", bits[-1])
    near, positives, got = tie((near, positives, got))
    far = swap(near, "dp", 1)
    own_docs = prepare(positives[0], positive_lengths)
    parts = [got]
    held = jnp.concatenate([own_rows, got], axis=0)
    crossed = []
    for n, bit in enumerate(reversed(bits[1:-1])):
        got = swap(held, "dp", bit)
        crossed.append(swap(held if n == 0 else parts[-1], "dp", last))
        if n == 0:
            got, own_docs = tie((got, own_docs))
        parts.append(got)
        held = jnp.concatenate([held, got], axis=0)
    other_docs = jnp.concatenate(
        [
            lax.ppermute(own_docs, "blk", [(i, (i + k) % groups) for i in range(groups)])
            for k in range(1, groups)
        ],
        axis=0,
    )
    early_cross = score(crossed, near, far, qlen)
    late_cross = swap(parts[-1], "dp", last)
    late_cross, early_cross = tie((late_cross, early_cross))
    late_cross = score([late_cross], near, far, qlen)

    gate = jnp.concatenate([early_cross, late_cross], axis=0)
    arrived = swap(gate[None], "dp", last)
    back = arrived
    for n, bit in enumerate(bits[1:]):
        half = back.shape[1] // 2
        rows = [parts[-1 - n]] if n < len(bits) - 2 else [own_rows, parts[0]]
        rows, gate = tie((rows, gate))
        mine = score(rows, near, far, qlen)
        arrived, mine = tie((arrived, mine))
        if n == 0:
            back = arrived
        gate = arrived
        leaving = jnp.concatenate([mine[None, -half:], back[:, half:]], axis=0)
        if n == len(bits) - 2:
            leaving, other_docs, owners = tie((leaving, other_docs, owners))
            apart = owners[0, :, :, 0] ^ me
            odd = functools.reduce(lambda x, m: x ^ (apart >> m), range(1, peers.bit_length() - 1), apart) & 1
            lane = odd * pass_count + local_ids[0]
            teach, index = teach_rows(apart >> 1, lane, teacher, query_count * qlen)
            contrast = contrast_loss(own_rows[0], own_docs, other_docs, qlen)
        arrived = swap(leaving, "dp", bit)
        if n == len(bits) - 2:
            arrived, contrast, teach = tie((arrived, contrast, teach))
        back = jnp.concatenate([back[:, :half], arrived], axis=0)
    returned = jnp.concatenate([mine[:1], back[:, 0]], axis=0)
    student, distill = distill_loss(returned, teach, index, teacher.shape)
    return (student, distill, contrast)


def solution(mesh):
    in_specs = (
        P("blk", "dp", None, None),
        P("blk", "dp", None, None),
        P("blk", "dp"),
        P("blk", "dp", None, None),
        P("blk", "dp"),
        P("blk", "dp", None, None),
        P("blk", "dp", None),
        P("blk", "dp", None),
    )
    out_specs = (P("blk", "dp", None), P("blk", "dp"), P("blk", "dp"))
    return jax.shard_map(
        per_device, mesh=mesh, in_specs=in_specs, out_specs=out_specs, check_vma=False
    )
```

```python
import functools

import jax
import jax.numpy as jnp
from jax import lax
from jax.experimental import pallas as pl
from jax.experimental.pallas import tpu as pltpu
from jax.sharding import PartitionSpec as P

VMEM = pl.BlockSpec(memory_space=pltpu.VMEM)
SMEM = pl.BlockSpec(memory_space=pltpu.SMEM)
LIMIT = 32 * 1024 * 1024


def unit(values):
    wide = values.astype(jnp.float32)
    total = jnp.sum(wide * wide, axis=-1, keepdims=True) + 1e-06
    return (wide * lax.rsqrt(total)).astype(jnp.bfloat16)


def kept_unit(rows, kept):
    place = lax.broadcasted_iota(jnp.int32, (rows.shape[0], 1), 0)
    wide = rows.astype(jnp.float32)
    return unit(jnp.where(place < kept, wide, wide[0:1]))


def group_sum(values, width, packed=False):
    lanes = values.shape[1]
    row = lax.broadcasted_iota(jnp.int32, (lanes, lanes), 0) // width
    column = lax.broadcasted_iota(jnp.int32, (lanes, lanes), 1)
    column = column if packed else column // width
    same = (row == column).astype(jnp.bfloat16)
    high = values.astype(jnp.bfloat16)
    rest = values - high.astype(jnp.float32)
    middle = rest.astype(jnp.bfloat16)
    low = (rest - middle.astype(jnp.float32)).astype(jnp.bfloat16)
    stacked = jnp.concatenate([high, middle, low], axis=0)
    sums = jnp.dot(stacked, same, preferred_element_type=jnp.float32)
    count = values.shape[0]
    return sums[:count] + (sums[count : 2 * count] + sums[2 * count :])


def best_match(tokens, query_rows):
    similar = lax.dot_general(
        tokens, query_rows, (((1,), (1,)), ((), ())), preferred_element_type=jnp.float32
    )
    return jnp.max(similar, axis=0, keepdims=True)


def prepare_kernel(kept_ref, rows_ref, out_ref):
    def one(i, carry):
        out_ref[i] = kept_unit(rows_ref[i], kept_ref[0, i])
        return carry

    lax.fori_loop(0, rows_ref.shape[0], one, 0, unroll=4)


def prepare(rows, kept):
    return pl.pallas_call(
        prepare_kernel,
        out_shape=jax.ShapeDtypeStruct(rows.shape, rows.dtype),
        in_specs=[SMEM, VMEM],
        out_specs=VMEM,
        compiler_params=pltpu.CompilerParams(vmem_limit_bytes=LIMIT),
        cost_estimate=pl.CostEstimate(flops=16 * rows.size, bytes_accessed=4 * rows.size, transcendentals=0),
    )(kept, rows)


def flat_lanes(rows, pad_ref, lanes):
    queries, width = rows.shape
    pad_ref[:queries, :width] = rows
    place = lax.broadcasted_iota(jnp.int32, (8, lanes), 1)
    spread = jnp.take_along_axis(pad_ref[...], place % width, axis=1)
    row = lax.broadcasted_iota(jnp.int32, (8, lanes), 0)
    return jnp.sum(jnp.where(row == place // width, spread, 0), axis=0, keepdims=True)


def prepare_docs_kernel(width, kept_ref, rows_ref, teacher_ref, out_ref, teach_ref, pad_ref):
    prepare_kernel(kept_ref, rows_ref, out_ref)
    teacher = flat_lanes(teacher_ref[0], pad_ref, teach_ref.shape[1])
    log_teacher = teacher - jnp.log(group_sum(jnp.exp(teacher), width))
    share = jnp.exp(log_teacher)
    teach_ref[0:1, :] = share
    teach_ref[1:3, :] = group_sum(jnp.concatenate([share * log_teacher, share], axis=0), width, packed=True)


def prepare_docs(rows, kept, teacher, lanes):
    return pl.pallas_call(
        functools.partial(prepare_docs_kernel, teacher.shape[2]),
        out_shape=(
            jax.ShapeDtypeStruct(rows.shape, rows.dtype),
            jax.ShapeDtypeStruct((3, lanes), jnp.float32),
        ),
        in_specs=[SMEM, VMEM, VMEM],
        out_specs=(VMEM, VMEM),
        scratch_shapes=[pltpu.VMEM((8, lanes), jnp.float32)],
        compiler_params=pltpu.CompilerParams(vmem_limit_bytes=LIMIT),
        cost_estimate=pl.CostEstimate(flops=16 * rows.size, bytes_accessed=4 * rows.size, transcendentals=0),
    )(kept, rows, teacher)


def score_kernel(qlen, count, *refs):
    query_refs, (near_ref, far_ref, out_ref, best_ref) = refs[:count], refs[count:]
    near = near_ref.shape[0]
    total = near + far_ref.shape[0]
    lanes = query_refs[0].shape[1]
    row = lax.broadcasted_iota(jnp.int32, (total, lanes), 0)
    column = lax.broadcasted_iota(jnp.int32, (total, lanes), 1) % qlen
    start = 0
    queries = [ref[i] for ref in query_refs for i in range(ref.shape[0])]
    while start < len(queries):
        block = [unit(q) for q in queries[start : start + 2]]
        joined = jnp.concatenate(block, axis=0)
        width = joined.shape[0]
        for i in range(total):
            tokens = near_ref[i] if i < near else far_ref[i - near]
            best_ref[i : i + 1, :width] = best_match(tokens, joined)
        for s in range(len(block)):
            summed = group_sum(best_ref[:, s * lanes : (s + 1) * lanes], qlen)
            out_ref[start + s : start + s + 1, :] = jnp.sum(
                jnp.where(row == column, summed, 0.0), axis=0, keepdims=True
            )
        start += 2


def score(query_list, near, far, qlen):
    lanes = query_list[0].shape[1]
    sources = sum(q.shape[0] for q in query_list)
    total = near.shape[0] + far.shape[0]
    return pl.pallas_call(
        functools.partial(score_kernel, qlen, len(query_list)),
        out_shape=jax.ShapeDtypeStruct((sources, lanes), jnp.float32),
        in_specs=[VMEM] * (len(query_list) + 2),
        out_specs=VMEM,
        scratch_shapes=[pltpu.VMEM((total, 2 * lanes), jnp.float32)],
        compiler_params=pltpu.CompilerParams(vmem_limit_bytes=LIMIT),
        cost_estimate=pl.CostEstimate(
            flops=2 * sources * lanes * near.shape[2] * total * near.shape[1],
            bytes_accessed=2 * (near.size + far.size),
            transcendentals=0,
        ),
    )(*query_list, near, far)


def contrast_kernel(
    qlen, query_ref, own_ref, other_ref, where_ref, lane_ref, contrast_ref, index_ref, best_ref, ints_ref
):
    queries = unit(query_ref[...])
    lanes = queries.shape[0]
    docs = own_ref.shape[0]
    total = docs + other_ref.shape[0]
    for i in range(total):
        tokens = own_ref[i] if i < docs else other_ref[i - docs]
        best_ref[i : i + 1, :] = best_match(tokens, queries)
    count, width = where_ref.shape
    index_ref[0:1, :] = flat_lanes(where_ref[...], ints_ref.at[0], lanes)
    lane = flat_lanes(lane_ref[...], ints_ref.at[1], lanes)
    index_ref[1:2, :] = lane + lax.broadcasted_iota(jnp.int32, (1, lanes), 1) // width * (lanes // count)
    logits = group_sum(best_ref[...], qlen)
    row = lax.broadcasted_iota(jnp.int32, (total, lanes), 0)
    query = lax.broadcasted_iota(jnp.int32, (total, lanes), 1) // qlen
    own = jnp.sum(jnp.where(row == query, logits, 0.0), axis=0, keepdims=True)
    loss = jnp.log(jnp.sum(jnp.exp(logits), axis=0, keepdims=True)) - own
    place = (lax.broadcasted_iota(jnp.int32, (8, lanes), 1) * qlen) % lanes
    spread = jnp.take_along_axis(jnp.broadcast_to(loss, (8, lanes)), place, axis=1)
    contrast_ref[...] = spread[0:1, : lanes // qlen]


def contrast_loss(query_rows, own, other, whose, lane, qlen):
    lanes = query_rows.shape[0]
    total = own.shape[0] + other.shape[0]
    return pl.pallas_call(
        functools.partial(contrast_kernel, qlen),
        out_shape=(
            jax.ShapeDtypeStruct((1, lanes // qlen), jnp.float32),
            jax.ShapeDtypeStruct((2, lanes), jnp.int32),
        ),
        in_specs=[VMEM] * 5,
        out_specs=(VMEM, VMEM),
        scratch_shapes=[pltpu.VMEM((total, lanes), jnp.float32), pltpu.VMEM((2, 8, lanes), jnp.int32)],
        compiler_params=pltpu.CompilerParams(vmem_limit_bytes=LIMIT),
        cost_estimate=pl.CostEstimate(
            flops=2 * lanes * own.shape[2] * total * own.shape[1], bytes_accessed=4 * own.size, transcendentals=0
        ),
    )(query_rows, own, other, whose, lane)


def distill_kernel(returned_ref, teach_ref, index_ref, student_ref, distill_ref):
    queries, width = student_ref.shape[1:]
    scorers, lanes = returned_ref.shape
    picked = jnp.take_along_axis(
        returned_ref[...], jnp.broadcast_to(index_ref[1:2, :], (scorers, lanes)), axis=1
    )
    row = lax.broadcasted_iota(jnp.int32, (scorers, lanes), 0)
    student = jnp.sum(jnp.where(row == index_ref[0:1, :], picked, 0.0), axis=0, keepdims=True)
    first = lax.broadcasted_iota(jnp.int32, (8, lanes), 0)
    place = lax.broadcasted_iota(jnp.int32, (8, lanes), 1)
    spread = jnp.take_along_axis(jnp.broadcast_to(student, (8, lanes)), (first * width + place) % lanes, axis=1)
    student_ref[0] = spread[:queries, :width]
    share = teach_ref[0:1, :]
    sums = group_sum(jnp.concatenate([jnp.exp(student), share * student], axis=0), width, packed=True)
    loss = teach_ref[1:2, :] - sums[1:2] + teach_ref[2:3, :] * jnp.log(sums[0:1])
    distill_ref[...] = loss[:, :queries]


def distill_loss(returned, teach, index, shape):
    return pl.pallas_call(
        distill_kernel,
        out_shape=(
            jax.ShapeDtypeStruct(shape, jnp.float32),
            jax.ShapeDtypeStruct(shape[:2], jnp.float32),
        ),
        in_specs=[VMEM] * 3,
        out_specs=(VMEM, VMEM),
        compiler_params=pltpu.CompilerParams(vmem_limit_bytes=LIMIT),
    )(returned, teach, index)


def swap(values, axis, bit):
    return lax.ppermute(values, axis, [(i, i ^ bit) for i in range(lax.axis_size(axis))])


def per_device(
    queries, passages, passage_lengths, positives, positive_lengths, owners, local_ids, teacher
):
    peers = lax.axis_size("dp")
    groups = lax.axis_size("blk")
    me = lax.axis_index("dp")
    query_count, qlen = queries.shape[1:3]
    pass_count = passages.shape[1]
    own_rows = queries.reshape(1, query_count * qlen, queries.shape[3])
    bits = [(1 << n) | 1 for n in range(1, peers.bit_length() - 1)]

    tie = lax.optimization_barrier

    last = bits[0]
    near = prepare(passages[0], passage_lengths)
    got = swap(own_rows, "dp", bits[-1])
    near, positives, got = tie((near, positives, got))
    far = swap(near, "dp", 1)
    own_docs, teach = prepare_docs(positives[0], positive_lengths, teacher, query_count * qlen)
    parts = [got]
    held = jnp.concatenate([own_rows, got], axis=0)
    crossed = []
    for n, bit in enumerate(reversed(bits[1:-1])):
        got = swap(held, "dp", bit)
        crossed.append(swap(held if n == 0 else parts[-1], "dp", last))
        if n == 0:
            got, own_docs, teach = tie((got, own_docs, teach))
        parts.append(got)
        held = jnp.concatenate([held, got], axis=0)
    other_docs = jnp.concatenate(
        [
            lax.ppermute(own_docs, "blk", [(i, (i + k) % groups) for i in range(groups)])
            for k in range(1, groups)
        ],
        axis=0,
    )
    early_cross = score(crossed, near, far, qlen)
    late_cross = swap(parts[-1], "dp", last)
    late_cross, early_cross = tie((late_cross, early_cross))
    late_cross = score([late_cross], near, far, qlen)

    gate = jnp.concatenate([early_cross, late_cross], axis=0)
    arrived = swap(gate[None], "dp", last)
    back = arrived
    for n, bit in enumerate(bits[1:]):
        half = back.shape[1] // 2
        rows = [parts[-1 - n]] if n < len(bits) - 2 else [own_rows, parts[0]]
        rows, gate = tie((rows, gate))
        mine = score(rows, near, far, qlen)
        arrived, mine = tie((arrived, mine))
        if n == 0:
            back = arrived
        gate = arrived
        leaving = jnp.concatenate([mine[None, -half:], back[:, half:]], axis=0)
        if n == len(bits) - 2:
            leaving, other_docs, owners = tie((leaving, other_docs, owners))
            apart = owners[0, :, :, 0] ^ me
            odd = functools.reduce(lambda x, m: x ^ (apart >> m), range(1, peers.bit_length() - 1), apart) & 1
            lane = odd * pass_count + local_ids[0]
            contrast, index = contrast_loss(own_rows[0], own_docs, other_docs, apart >> 1, lane, qlen)
        arrived = swap(leaving, "dp", bit)
        if n == len(bits) - 2:
            arrived, contrast, index = tie((arrived, contrast, index))
        back = jnp.concatenate([back[:, :half], arrived], axis=0)
    returned = jnp.concatenate([mine[:1], back[:, 0]], axis=0)
    student, distill = distill_loss(returned, teach, index, teacher.shape)
    return (student, distill, contrast)


def solution(mesh):
    in_specs = (
        P("blk", "dp", None, None),
        P("blk", "dp", None, None),
        P("blk", "dp"),
        P("blk", "dp", None, None),
        P("blk", "dp"),
        P("blk", "dp", None, None),
        P("blk", "dp", None),
        P("blk", "dp", None),
    )
    out_specs = (P("blk", "dp", None), P("blk", "dp"), P("blk", "dp"))
    return jax.shard_map(
        per_device, mesh=mesh, in_specs=in_specs, out_specs=out_specs, check_vma=False
    )
```

```python
import functools

import jax
import jax.numpy as jnp
from jax import lax
from jax.experimental import pallas as pl
from jax.experimental.pallas import tpu as pltpu
from jax.sharding import PartitionSpec as P

VMEM = pl.BlockSpec(memory_space=pltpu.VMEM)
SMEM = pl.BlockSpec(memory_space=pltpu.SMEM)
LIMIT = 32 * 1024 * 1024


def unit(values):
    wide = values.astype(jnp.float32)
    total = jnp.sum(wide * wide, axis=-1, keepdims=True) + 1e-06
    return (wide * lax.rsqrt(total)).astype(jnp.bfloat16)


def kept_unit(rows, kept):
    place = lax.broadcasted_iota(jnp.int32, (rows.shape[0], 1), 0)
    wide = rows.astype(jnp.float32)
    return unit(jnp.where(place < kept, wide, wide[0:1]))


def group_sum(values, width, packed=False):
    lanes = values.shape[1]
    row = lax.broadcasted_iota(jnp.int32, (lanes, lanes), 0) // width
    column = lax.broadcasted_iota(jnp.int32, (lanes, lanes), 1)
    column = column if packed else column // width
    same = (row == column).astype(jnp.bfloat16)
    high = values.astype(jnp.bfloat16)
    rest = values - high.astype(jnp.float32)
    middle = rest.astype(jnp.bfloat16)
    low = (rest - middle.astype(jnp.float32)).astype(jnp.bfloat16)
    stacked = jnp.concatenate([high, middle, low], axis=0)
    sums = jnp.dot(stacked, same, preferred_element_type=jnp.float32)
    count = values.shape[0]
    return sums[:count] + (sums[count : 2 * count] + sums[2 * count :])


def best_match(tokens, query_rows):
    similar = lax.dot_general(
        tokens, query_rows, (((1,), (1,)), ((), ())), preferred_element_type=jnp.float32
    )
    return jnp.max(similar, axis=0, keepdims=True)


def prepare_kernel(kept_ref, rows_ref, out_ref):
    def one(i, carry):
        out_ref[i] = kept_unit(rows_ref[i], kept_ref[0, i])
        return carry

    lax.fori_loop(0, rows_ref.shape[0], one, 0, unroll=4)


def prepare(rows, kept):
    return pl.pallas_call(
        prepare_kernel,
        out_shape=jax.ShapeDtypeStruct(rows.shape, rows.dtype),
        in_specs=[SMEM, VMEM],
        out_specs=VMEM,
        compiler_params=pltpu.CompilerParams(vmem_limit_bytes=LIMIT),
        cost_estimate=pl.CostEstimate(flops=16 * rows.size, bytes_accessed=4 * rows.size, transcendentals=0),
    )(kept, rows)


def flat_lanes(rows, pad_ref, lanes):
    queries, width = rows.shape
    pad_ref[:queries, :width] = rows
    place = lax.broadcasted_iota(jnp.int32, (8, lanes), 1)
    spread = jnp.take_along_axis(pad_ref[...], place % width, axis=1)
    row = lax.broadcasted_iota(jnp.int32, (8, lanes), 0)
    return jnp.sum(jnp.where(row == place // width, spread, 0), axis=0, keepdims=True)


def prepare_docs_kernel(width, kept_ref, rows_ref, teacher_ref, out_ref, teach_ref, pad_ref):
    prepare_kernel(kept_ref, rows_ref, out_ref)
    teacher = flat_lanes(teacher_ref[0], pad_ref, teach_ref.shape[1])
    log_teacher = teacher - jnp.log(group_sum(jnp.exp(teacher), width))
    share = jnp.exp(log_teacher)
    teach_ref[0:1, :] = share
    teach_ref[1:3, :] = group_sum(jnp.concatenate([share * log_teacher, share], axis=0), width, packed=True)


def prepare_docs(rows, kept, teacher, lanes):
    return pl.pallas_call(
        functools.partial(prepare_docs_kernel, teacher.shape[2]),
        out_shape=(
            jax.ShapeDtypeStruct(rows.shape, rows.dtype),
            jax.ShapeDtypeStruct((3, lanes), jnp.float32),
        ),
        in_specs=[SMEM, VMEM, VMEM],
        out_specs=(VMEM, VMEM),
        scratch_shapes=[pltpu.VMEM((8, lanes), jnp.float32)],
        compiler_params=pltpu.CompilerParams(vmem_limit_bytes=LIMIT),
        cost_estimate=pl.CostEstimate(flops=160000 * rows.size, bytes_accessed=4 * rows.size, transcendentals=0),
    )(kept, rows, teacher)


def score_kernel(qlen, count, *refs):
    query_refs, (near_ref, far_ref, out_ref, best_ref) = refs[:count], refs[count:]
    near = near_ref.shape[0]
    total = near + far_ref.shape[0]
    lanes = query_refs[0].shape[1]
    row = lax.broadcasted_iota(jnp.int32, (total, lanes), 0)
    column = lax.broadcasted_iota(jnp.int32, (total, lanes), 1) % qlen
    start = 0
    queries = [ref[i] for ref in query_refs for i in range(ref.shape[0])]
    while start < len(queries):
        block = [unit(q) for q in queries[start : start + 2]]
        joined = jnp.concatenate(block, axis=0)
        width = joined.shape[0]
        for i in range(total):
            tokens = near_ref[i] if i < near else far_ref[i - near]
            best_ref[i : i + 1, :width] = best_match(tokens, joined)
        both = jnp.concatenate([best_ref[:, s * lanes : (s + 1) * lanes] for s in range(len(block))], axis=0)
        summed = group_sum(both, qlen)
        for s in range(len(block)):
            out_ref[start + s : start + s + 1, :] = jnp.sum(
                jnp.where(row == column, summed[s * total : (s + 1) * total], 0.0), axis=0, keepdims=True
            )
        start += 2


def score(query_list, near, far, qlen):
    lanes = query_list[0].shape[1]
    sources = sum(q.shape[0] for q in query_list)
    total = near.shape[0] + far.shape[0]
    return pl.pallas_call(
        functools.partial(score_kernel, qlen, len(query_list)),
        out_shape=jax.ShapeDtypeStruct((sources, lanes), jnp.float32),
        in_specs=[VMEM] * (len(query_list) + 2),
        out_specs=VMEM,
        scratch_shapes=[pltpu.VMEM((total, 2 * lanes), jnp.float32)],
        compiler_params=pltpu.CompilerParams(vmem_limit_bytes=LIMIT),
        cost_estimate=pl.CostEstimate(
            flops=2 * sources * lanes * near.shape[2] * total * near.shape[1],
            bytes_accessed=2 * (near.size + far.size),
            transcendentals=0,
        ),
    )(*query_list, near, far)


def contrast_kernel(
    qlen, query_ref, own_ref, other_ref, where_ref, lane_ref, contrast_ref, index_ref, best_ref, ints_ref
):
    queries = unit(query_ref[...])
    lanes = queries.shape[0]
    docs = own_ref.shape[0]
    total = docs + other_ref.shape[0]
    for i in range(total):
        tokens = own_ref[i] if i < docs else other_ref[i - docs]
        best_ref[i : i + 1, :] = best_match(tokens, queries)
    count, width = where_ref.shape
    index_ref[0:1, :] = flat_lanes(where_ref[...], ints_ref.at[0], lanes)
    lane = flat_lanes(lane_ref[...], ints_ref.at[1], lanes)
    index_ref[1:2, :] = lane + lax.broadcasted_iota(jnp.int32, (1, lanes), 1) // width * (lanes // count)
    logits = group_sum(best_ref[...], qlen)
    row = lax.broadcasted_iota(jnp.int32, (total, lanes), 0)
    query = lax.broadcasted_iota(jnp.int32, (total, lanes), 1) // qlen
    own = jnp.sum(jnp.where(row == query, logits, 0.0), axis=0, keepdims=True)
    loss = jnp.log(jnp.sum(jnp.exp(logits), axis=0, keepdims=True)) - own
    place = (lax.broadcasted_iota(jnp.int32, (8, lanes), 1) * qlen) % lanes
    spread = jnp.take_along_axis(jnp.broadcast_to(loss, (8, lanes)), place, axis=1)
    contrast_ref[...] = spread[0:1, : lanes // qlen]


def contrast_loss(query_rows, own, other, whose, lane, qlen):
    lanes = query_rows.shape[0]
    total = own.shape[0] + other.shape[0]
    return pl.pallas_call(
        functools.partial(contrast_kernel, qlen),
        out_shape=(
            jax.ShapeDtypeStruct((1, lanes // qlen), jnp.float32),
            jax.ShapeDtypeStruct((2, lanes), jnp.int32),
        ),
        in_specs=[VMEM] * 5,
        out_specs=(VMEM, VMEM),
        scratch_shapes=[pltpu.VMEM((total, lanes), jnp.float32), pltpu.VMEM((2, 8, lanes), jnp.int32)],
        compiler_params=pltpu.CompilerParams(vmem_limit_bytes=LIMIT),
        cost_estimate=pl.CostEstimate(
            flops=2 * lanes * own.shape[2] * total * own.shape[1], bytes_accessed=4 * own.size, transcendentals=0
        ),
    )(query_rows, own, other, whose, lane)


def distill_kernel(returned_ref, teach_ref, index_ref, student_ref, distill_ref):
    queries, width = student_ref.shape[1:]
    scorers, lanes = returned_ref.shape
    picked = jnp.take_along_axis(
        returned_ref[...], jnp.broadcast_to(index_ref[1:2, :], (scorers, lanes)), axis=1
    )
    row = lax.broadcasted_iota(jnp.int32, (scorers, lanes), 0)
    student = jnp.sum(jnp.where(row == index_ref[0:1, :], picked, 0.0), axis=0, keepdims=True)
    first = lax.broadcasted_iota(jnp.int32, (8, lanes), 0)
    place = lax.broadcasted_iota(jnp.int32, (8, lanes), 1)
    spread = jnp.take_along_axis(jnp.broadcast_to(student, (8, lanes)), (first * width + place) % lanes, axis=1)
    student_ref[0] = spread[:queries, :width]
    share = teach_ref[0:1, :]
    sums = group_sum(jnp.concatenate([jnp.exp(student), share * student], axis=0), width, packed=True)
    loss = teach_ref[1:2, :] - sums[1:2] + teach_ref[2:3, :] * jnp.log(sums[0:1])
    distill_ref[...] = loss[:, :queries]


def distill_loss(returned, teach, index, shape):
    return pl.pallas_call(
        distill_kernel,
        out_shape=(
            jax.ShapeDtypeStruct(shape, jnp.float32),
            jax.ShapeDtypeStruct(shape[:2], jnp.float32),
        ),
        in_specs=[VMEM] * 3,
        out_specs=(VMEM, VMEM),
        compiler_params=pltpu.CompilerParams(vmem_limit_bytes=LIMIT),
    )(returned, teach, index)


def swap(values, axis, bit):
    return lax.ppermute(values, axis, [(i, i ^ bit) for i in range(lax.axis_size(axis))])


def per_device(
    queries, passages, passage_lengths, positives, positive_lengths, owners, local_ids, teacher
):
    peers = lax.axis_size("dp")
    groups = lax.axis_size("blk")
    me = lax.axis_index("dp")
    query_count, qlen = queries.shape[1:3]
    pass_count = passages.shape[1]
    own_rows = queries.reshape(1, query_count * qlen, queries.shape[3])
    bits = [(1 << n) | 1 for n in range(1, peers.bit_length() - 1)]

    tie = lax.optimization_barrier

    last = bits[0]
    near = prepare(passages[0], passage_lengths)
    got = swap(own_rows, "dp", bits[-1])
    positives, got = tie((positives, got))
    far = swap(near, "dp", 1)
    own_docs, teach = prepare_docs(positives[0], positive_lengths, teacher, query_count * qlen)
    parts = [got]
    held = jnp.concatenate([own_rows, got], axis=0)
    crossed = []
    for n, bit in enumerate(reversed(bits[1:-1])):
        got = swap(held, "dp", bit)
        crossing = held if n == 0 else parts[-1]
        if n == 0:
            crossing, own_docs = tie((crossing, own_docs))
        crossed.append(swap(crossing, "dp", last))
        if n == 0:
            got, own_docs, teach = tie((got, own_docs, teach))
        parts.append(got)
        held = jnp.concatenate([held, got], axis=0)
    other_docs = jnp.concatenate(
        [
            lax.ppermute(own_docs, "blk", [(i, (i + k) % groups) for i in range(groups)])
            for k in range(1, groups)
        ],
        axis=0,
    )
    early_cross = score(crossed, near, far, qlen)
    late_cross = swap(parts[-1], "dp", last)
    late_cross, early_cross = tie((late_cross, early_cross))
    late_cross = score([late_cross], near, far, qlen)

    gate = jnp.concatenate([early_cross, late_cross], axis=0)
    arrived = swap(gate[None], "dp", last)
    back = arrived
    for n, bit in enumerate(bits[1:]):
        half = back.shape[1] // 2
        rows = [parts[-1 - n]] if n < len(bits) - 2 else [own_rows, parts[0]]
        rows, gate = tie((rows, gate))
        mine = score(rows, near, far, qlen)
        arrived, mine = tie((arrived, mine))
        if n == 0:
            back = arrived
        gate = arrived
        leaving = jnp.concatenate([mine[None, -half:], back[:, half:]], axis=0)
        if n == len(bits) - 2:
            leaving, other_docs, owners = tie((leaving, other_docs, owners))
            apart = owners[0, :, :, 0] ^ me
            odd = functools.reduce(lambda x, m: x ^ (apart >> m), range(1, peers.bit_length() - 1), apart) & 1
            lane = odd * pass_count + local_ids[0]
            contrast, index = contrast_loss(own_rows[0], own_docs, other_docs, apart >> 1, lane, qlen)
        arrived = swap(leaving, "dp", bit)
        if n == len(bits) - 2:
            arrived, contrast, index = tie((arrived, contrast, index))
        back = jnp.concatenate([back[:, :half], arrived], axis=0)
    returned = jnp.concatenate([mine[:1], back[:, 0]], axis=0)
    student, distill = distill_loss(returned, teach, index, teacher.shape)
    return (student, distill, contrast)


def solution(mesh):
    in_specs = (
        P("blk", "dp", None, None),
        P("blk", "dp", None, None),
        P("blk", "dp"),
        P("blk", "dp", None, None),
        P("blk", "dp"),
        P("blk", "dp", None, None),
        P("blk", "dp", None),
        P("blk", "dp", None),
    )
    out_specs = (P("blk", "dp", None), P("blk", "dp"), P("blk", "dp"))
    return jax.shard_map(
        per_device, mesh=mesh, in_specs=in_specs, out_specs=out_specs, check_vma=False
    )
```

```python
import functools

import jax
import jax.numpy as jnp
from jax import lax
from jax.experimental import pallas as pl
from jax.experimental.pallas import tpu as pltpu
from jax.sharding import PartitionSpec as P

VMEM = pl.BlockSpec(memory_space=pltpu.VMEM)
SMEM = pl.BlockSpec(memory_space=pltpu.SMEM)
LIMIT = 32 * 1024 * 1024


def unit(values):
    wide = values.astype(jnp.float32)
    total = jnp.sum(wide * wide, axis=-1, keepdims=True) + 1e-06
    return (wide * lax.rsqrt(total)).astype(jnp.bfloat16)


def kept_unit(rows, kept):
    place = lax.broadcasted_iota(jnp.int32, (rows.shape[0], 1), 0)
    wide = rows.astype(jnp.float32)
    return unit(jnp.where(place < kept, wide, wide[0:1]))


def group_sum(values, width, packed=False):
    lanes = values.shape[1]
    row = lax.broadcasted_iota(jnp.int32, (lanes, lanes), 0) // width
    column = lax.broadcasted_iota(jnp.int32, (lanes, lanes), 1)
    column = column if packed else column // width
    same = (row == column).astype(jnp.bfloat16)
    high = values.astype(jnp.bfloat16)
    rest = values - high.astype(jnp.float32)
    middle = rest.astype(jnp.bfloat16)
    low = (rest - middle.astype(jnp.float32)).astype(jnp.bfloat16)
    stacked = jnp.concatenate([high, middle, low], axis=0)
    sums = jnp.dot(stacked, same, preferred_element_type=jnp.float32)
    count = values.shape[0]
    return sums[:count] + (sums[count : 2 * count] + sums[2 * count :])


def best_match(tokens, query_rows):
    similar = lax.dot_general(
        tokens, query_rows, (((1,), (1,)), ((), ())), preferred_element_type=jnp.float32
    )
    return jnp.max(similar, axis=0, keepdims=True)


def prepare_kernel(kept_ref, rows_ref, out_ref):
    def one(i, carry):
        out_ref[i] = kept_unit(rows_ref[i], kept_ref[0, i])
        return carry

    lax.fori_loop(0, rows_ref.shape[0], one, 0, unroll=rows_ref.shape[0])


def prepare(rows, kept):
    return pl.pallas_call(
        prepare_kernel,
        out_shape=jax.ShapeDtypeStruct(rows.shape, rows.dtype),
        in_specs=[SMEM, VMEM],
        out_specs=VMEM,
        compiler_params=pltpu.CompilerParams(vmem_limit_bytes=LIMIT),
        cost_estimate=pl.CostEstimate(flops=16 * rows.size, bytes_accessed=4 * rows.size, transcendentals=0),
    )(kept, rows)


def flat_lanes(rows, pad_ref, lanes):
    queries, width = rows.shape
    pad_ref[:queries, :width] = rows
    place = lax.broadcasted_iota(jnp.int32, (8, lanes), 1)
    spread = jnp.take_along_axis(pad_ref[...], place % width, axis=1)
    row = lax.broadcasted_iota(jnp.int32, (8, lanes), 0)
    return jnp.sum(jnp.where(row == place // width, spread, 0), axis=0, keepdims=True)


def prepare_docs_kernel(width, kept_ref, rows_ref, teacher_ref, out_ref, teach_ref, pad_ref):
    prepare_kernel(kept_ref, rows_ref, out_ref)
    teacher = flat_lanes(teacher_ref[0], pad_ref, teach_ref.shape[1])
    log_teacher = teacher - jnp.log(group_sum(jnp.exp(teacher), width))
    share = jnp.exp(log_teacher)
    teach_ref[0:1, :] = share
    teach_ref[1:3, :] = group_sum(jnp.concatenate([share * log_teacher, share], axis=0), width, packed=True)


def prepare_docs(rows, kept, teacher, lanes):
    return pl.pallas_call(
        functools.partial(prepare_docs_kernel, teacher.shape[2]),
        out_shape=(
            jax.ShapeDtypeStruct(rows.shape, rows.dtype),
            jax.ShapeDtypeStruct((3, lanes), jnp.float32),
        ),
        in_specs=[SMEM, VMEM, VMEM],
        out_specs=(VMEM, VMEM),
        scratch_shapes=[pltpu.VMEM((8, lanes), jnp.float32)],
        compiler_params=pltpu.CompilerParams(vmem_limit_bytes=LIMIT),
        cost_estimate=pl.CostEstimate(flops=160000 * rows.size, bytes_accessed=4 * rows.size, transcendentals=0),
    )(kept, rows, teacher)


def score_kernel(qlen, count, *refs):
    query_refs, (near_ref, far_ref, out_ref, best_ref) = refs[:count], refs[count:]
    near = near_ref.shape[0]
    total = near + far_ref.shape[0]
    lanes = query_refs[0].shape[1]
    row = lax.broadcasted_iota(jnp.int32, (total, lanes), 0)
    column = lax.broadcasted_iota(jnp.int32, (total, lanes), 1) % qlen
    start = 0
    queries = [ref[i] for ref in query_refs for i in range(ref.shape[0])]
    while start < len(queries):
        block = [unit(q) for q in queries[start : start + 2]]
        joined = jnp.concatenate(block, axis=0)
        width = joined.shape[0]
        for i in range(total):
            tokens = near_ref[i] if i < near else far_ref[i - near]
            best_ref[i : i + 1, :width] = best_match(tokens, joined)
        both = jnp.concatenate([best_ref[:, s * lanes : (s + 1) * lanes] for s in range(len(block))], axis=0)
        summed = group_sum(both, qlen)
        for s in range(len(block)):
            out_ref[start + s : start + s + 1, :] = jnp.sum(
                jnp.where(row == column, summed[s * total : (s + 1) * total], 0.0), axis=0, keepdims=True
            )
        start += 2


def score(query_list, near, far, qlen):
    lanes = query_list[0].shape[1]
    sources = sum(q.shape[0] for q in query_list)
    total = near.shape[0] + far.shape[0]
    return pl.pallas_call(
        functools.partial(score_kernel, qlen, len(query_list)),
        out_shape=jax.ShapeDtypeStruct((sources, lanes), jnp.float32),
        in_specs=[VMEM] * (len(query_list) + 2),
        out_specs=VMEM,
        scratch_shapes=[pltpu.VMEM((total, 2 * lanes), jnp.float32)],
        compiler_params=pltpu.CompilerParams(vmem_limit_bytes=LIMIT),
        cost_estimate=pl.CostEstimate(
            flops=2 * sources * lanes * near.shape[2] * total * near.shape[1],
            bytes_accessed=2 * (near.size + far.size),
            transcendentals=0,
        ),
    )(*query_list, near, far)


def contrast_kernel(
    qlen, query_ref, own_ref, other_ref, where_ref, lane_ref, contrast_ref, index_ref, best_ref, ints_ref
):
    queries = unit(query_ref[...])
    lanes = queries.shape[0]
    docs = own_ref.shape[0]
    total = docs + other_ref.shape[0]
    for i in range(total):
        tokens = own_ref[i] if i < docs else other_ref[i - docs]
        best_ref[i : i + 1, :] = best_match(tokens, queries)
    count, width = where_ref.shape
    index_ref[0:1, :] = flat_lanes(where_ref[...], ints_ref.at[0], lanes)
    lane = flat_lanes(lane_ref[...], ints_ref.at[1], lanes)
    index_ref[1:2, :] = lane + lax.broadcasted_iota(jnp.int32, (1, lanes), 1) // width * (lanes // count)
    logits = group_sum(best_ref[...], qlen)
    row = lax.broadcasted_iota(jnp.int32, (total, lanes), 0)
    query = lax.broadcasted_iota(jnp.int32, (total, lanes), 1) // qlen
    own = jnp.sum(jnp.where(row == query, logits, 0.0), axis=0, keepdims=True)
    loss = jnp.log(jnp.sum(jnp.exp(logits), axis=0, keepdims=True)) - own
    place = (lax.broadcasted_iota(jnp.int32, (8, lanes), 1) * qlen) % lanes
    spread = jnp.take_along_axis(jnp.broadcast_to(loss, (8, lanes)), place, axis=1)
    contrast_ref[...] = spread[0:1, : lanes // qlen]


def contrast_loss(query_rows, own, other, whose, lane, qlen):
    lanes = query_rows.shape[0]
    total = own.shape[0] + other.shape[0]
    return pl.pallas_call(
        functools.partial(contrast_kernel, qlen),
        out_shape=(
            jax.ShapeDtypeStruct((1, lanes // qlen), jnp.float32),
            jax.ShapeDtypeStruct((2, lanes), jnp.int32),
        ),
        in_specs=[VMEM] * 5,
        out_specs=(VMEM, VMEM),
        scratch_shapes=[pltpu.VMEM((total, lanes), jnp.float32), pltpu.VMEM((2, 8, lanes), jnp.int32)],
        compiler_params=pltpu.CompilerParams(vmem_limit_bytes=LIMIT),
        cost_estimate=pl.CostEstimate(
            flops=2 * lanes * own.shape[2] * total * own.shape[1], bytes_accessed=4 * own.size, transcendentals=0
        ),
    )(query_rows, own, other, whose, lane)


def distill_kernel(mine_ref, back_ref, teach_ref, index_ref, student_ref, distill_ref):
    queries, width = student_ref.shape[1:]
    scorers, lanes = 1 + back_ref.shape[0], back_ref.shape[1]
    returned = jnp.concatenate([mine_ref[...], back_ref[...]], axis=0)
    picked = jnp.take_along_axis(
        returned, jnp.broadcast_to(index_ref[1:2, :], (scorers, lanes)), axis=1
    )
    row = lax.broadcasted_iota(jnp.int32, (scorers, lanes), 0)
    student = jnp.sum(jnp.where(row == index_ref[0:1, :], picked, 0.0), axis=0, keepdims=True)
    first = lax.broadcasted_iota(jnp.int32, (8, lanes), 0)
    place = lax.broadcasted_iota(jnp.int32, (8, lanes), 1)
    spread = jnp.take_along_axis(jnp.broadcast_to(student, (8, lanes)), (first * width + place) % lanes, axis=1)
    student_ref[0] = spread[:queries, :width]
    share = teach_ref[0:1, :]
    sums = group_sum(jnp.concatenate([jnp.exp(student), share * student], axis=0), width, packed=True)
    loss = teach_ref[1:2, :] - sums[1:2] + teach_ref[2:3, :] * jnp.log(sums[0:1])
    distill_ref[...] = loss[:, :queries]


def distill_loss(returned, teach, index, shape):
    return pl.pallas_call(
        distill_kernel,
        out_shape=(
            jax.ShapeDtypeStruct(shape, jnp.float32),
            jax.ShapeDtypeStruct(shape[:2], jnp.float32),
        ),
        in_specs=[VMEM] * 4,
        out_specs=(VMEM, VMEM),
        compiler_params=pltpu.CompilerParams(vmem_limit_bytes=LIMIT),
    )(*returned, teach, index)


def swap(values, axis, bit):
    return lax.ppermute(values, axis, [(i, i ^ bit) for i in range(lax.axis_size(axis))])


def per_device(
    queries, passages, passage_lengths, positives, positive_lengths, owners, local_ids, teacher
):
    peers = lax.axis_size("dp")
    groups = lax.axis_size("blk")
    me = lax.axis_index("dp")
    query_count, qlen = queries.shape[1:3]
    pass_count = passages.shape[1]
    own_rows = queries.reshape(1, query_count * qlen, queries.shape[3])
    bits = [(1 << n) | 1 for n in range(1, peers.bit_length() - 1)]

    tie = lax.optimization_barrier

    last = bits[0]
    near = prepare(passages[0], passage_lengths)
    got = swap(own_rows, "dp", bits[-1])
    positives, got = tie((positives, got))
    far = swap(near, "dp", 1)
    own_docs, teach = prepare_docs(positives[0], positive_lengths, teacher, query_count * qlen)
    parts = [got]
    held = jnp.concatenate([own_rows, got], axis=0)
    crossed = []
    for n, bit in enumerate(reversed(bits[1:-1])):
        got = swap(held, "dp", bit)
        crossing = held if n == 0 else parts[-1]
        if n == 0:
            crossing, own_docs = tie((crossing, own_docs))
        crossed.append(swap(crossing, "dp", last))
        if n == 0:
            got, own_docs, teach = tie((got, own_docs, teach))
        parts.append(got)
        held = jnp.concatenate([held, got], axis=0)
    other_docs = jnp.concatenate(
        [
            lax.ppermute(own_docs, "blk", [(i, (i + k) % groups) for i in range(groups)])
            for k in range(1, groups)
        ],
        axis=0,
    )
    early_cross = score(crossed, near, far, qlen)
    late_cross = swap(parts[-1], "dp", last)
    late_cross, early_cross = tie((late_cross, early_cross))
    late_cross = score([late_cross], near, far, qlen)

    gate = jnp.concatenate([early_cross, late_cross], axis=0)
    arrived = swap(gate[None], "dp", last)
    back = arrived
    for n, bit in enumerate(bits[1:]):
        half = back.shape[1] // 2
        rows = [parts[-1 - n]] if n < len(bits) - 2 else [own_rows, parts[0]]
        rows, gate = tie((rows, gate))
        mine = score(rows, near, far, qlen)
        arrived, mine = tie((arrived, mine))
        if n == 0:
            back = arrived
        gate = arrived
        leaving = jnp.concatenate([mine[None, -half:], back[:, half:]], axis=0)
        if n == len(bits) - 2:
            leaving, other_docs, owners = tie((leaving, other_docs, owners))
            apart = owners[0, :, :, 0] ^ me
            odd = functools.reduce(lambda x, m: x ^ (apart >> m), range(1, peers.bit_length() - 1), apart) & 1
            lane = odd * pass_count + local_ids[0]
            contrast, index = contrast_loss(own_rows[0], own_docs, other_docs, apart >> 1, lane, qlen)
        arrived = swap(leaving, "dp", bit)
        if n == len(bits) - 2:
            arrived, contrast, index = tie((arrived, contrast, index))
        back = jnp.concatenate([back[:, :half], arrived], axis=0)
    returned = [mine[:1], back[:, 0]]
    student, distill = distill_loss(returned, teach, index, teacher.shape)
    return (student, distill, contrast)


def solution(mesh):
    in_specs = (
        P("blk", "dp", None, None),
        P("blk", "dp", None, None),
        P("blk", "dp"),
        P("blk", "dp", None, None),
        P("blk", "dp"),
        P("blk", "dp", None, None),
        P("blk", "dp", None),
        P("blk", "dp", None),
    )
    out_specs = (P("blk", "dp", None), P("blk", "dp"), P("blk", "dp"))
    return jax.shard_map(
        per_device, mesh=mesh, in_specs=in_specs, out_specs=out_specs, check_vma=False
    )
```

```python
import functools

import jax
import jax.numpy as jnp
from jax import lax
from jax.experimental import pallas as pl
from jax.experimental.pallas import tpu as pltpu
from jax.sharding import PartitionSpec as P

VMEM = pl.BlockSpec(memory_space=pltpu.VMEM)
SMEM = pl.BlockSpec(memory_space=pltpu.SMEM)
LIMIT = 32 * 1024 * 1024


def unit(values):
    wide = values.astype(jnp.float32)
    total = jnp.sum(wide * wide, axis=-1, keepdims=True) + 1e-06
    return (wide * lax.rsqrt(total)).astype(jnp.bfloat16)


def kept_unit(rows, kept):
    place = lax.broadcasted_iota(jnp.int32, (rows.shape[0], 1), 0)
    wide = rows.astype(jnp.float32)
    return unit(jnp.where(place < kept, wide, wide[0:1]))


def group_sum(values, width, packed=False):
    lanes = values.shape[1]
    row = lax.broadcasted_iota(jnp.int32, (lanes, lanes), 0) // width
    column = lax.broadcasted_iota(jnp.int32, (lanes, lanes), 1)
    column = column if packed else column // width
    same = (row == column).astype(jnp.bfloat16)
    high = values.astype(jnp.bfloat16)
    rest = values - high.astype(jnp.float32)
    middle = rest.astype(jnp.bfloat16)
    low = (rest - middle.astype(jnp.float32)).astype(jnp.bfloat16)
    stacked = jnp.concatenate([high, middle, low], axis=0)
    sums = jnp.dot(stacked, same, preferred_element_type=jnp.float32)
    count = values.shape[0]
    return sums[:count] + (sums[count : 2 * count] + sums[2 * count :])


def best_match(tokens, query_rows):
    similar = lax.dot_general(
        tokens, query_rows, (((1,), (1,)), ((), ())), preferred_element_type=jnp.float32
    )
    return jnp.max(similar, axis=0, keepdims=True)


def prepare_kernel(kept_ref, rows_ref, out_ref):
    def one(i, carry):
        out_ref[i] = kept_unit(rows_ref[i], kept_ref[0, i])
        return carry

    lax.fori_loop(0, rows_ref.shape[0], one, 0, unroll=rows_ref.shape[0])


def prepare(rows, kept):
    return pl.pallas_call(
        prepare_kernel,
        out_shape=jax.ShapeDtypeStruct(rows.shape, rows.dtype),
        in_specs=[SMEM, VMEM],
        out_specs=VMEM,
        compiler_params=pltpu.CompilerParams(vmem_limit_bytes=LIMIT),
        cost_estimate=pl.CostEstimate(flops=16 * rows.size, bytes_accessed=4 * rows.size, transcendentals=0),
    )(kept, rows)


def flat_lanes(rows, pad_ref, lanes):
    queries, width = rows.shape
    pad_ref[:queries, :width] = rows
    place = lax.broadcasted_iota(jnp.int32, (8, lanes), 1)
    spread = jnp.take_along_axis(pad_ref[...], place % width, axis=1)
    row = lax.broadcasted_iota(jnp.int32, (8, lanes), 0)
    return jnp.sum(jnp.where(row == place // width, spread, 0), axis=0, keepdims=True)


def prepare_docs_kernel(width, kept_ref, rows_ref, teacher_ref, out_ref, teach_ref, pad_ref):
    prepare_kernel(kept_ref, rows_ref, out_ref)
    teacher = flat_lanes(teacher_ref[0], pad_ref, teach_ref.shape[1])
    log_teacher = teacher - jnp.log(group_sum(jnp.exp(teacher), width))
    share = jnp.exp(log_teacher)
    teach_ref[0:1, :] = share
    teach_ref[1:3, :] = group_sum(jnp.concatenate([share * log_teacher, share], axis=0), width, packed=True)


def prepare_docs(rows, kept, teacher, lanes):
    return pl.pallas_call(
        functools.partial(prepare_docs_kernel, teacher.shape[2]),
        out_shape=(
            jax.ShapeDtypeStruct(rows.shape, rows.dtype),
            jax.ShapeDtypeStruct((3, lanes), jnp.float32),
        ),
        in_specs=[SMEM, VMEM, VMEM],
        out_specs=(VMEM, VMEM),
        scratch_shapes=[pltpu.VMEM((8, lanes), jnp.float32)],
        compiler_params=pltpu.CompilerParams(vmem_limit_bytes=LIMIT),
        cost_estimate=pl.CostEstimate(flops=160000 * rows.size, bytes_accessed=4 * rows.size, transcendentals=0),
    )(kept, rows, teacher)


def score_kernel(qlen, count, *refs):
    query_refs, (near_ref, far_ref, out_ref, best_ref) = refs[:count], refs[count:]
    near = near_ref.shape[0]
    total = near + far_ref.shape[0]
    lanes = query_refs[0].shape[1]
    row = lax.broadcasted_iota(jnp.int32, (total, lanes), 0)
    column = lax.broadcasted_iota(jnp.int32, (total, lanes), 1) % qlen
    start = 0
    queries = [ref[i] for ref in query_refs for i in range(ref.shape[0])]
    while start < len(queries):
        block = [unit(q) for q in queries[start : start + 2]]
        joined = jnp.concatenate(block, axis=0)
        width = joined.shape[0]
        for i in range(total):
            tokens = near_ref[i] if i < near else far_ref[i - near]
            best_ref[i : i + 1, :width] = best_match(tokens, joined)
        both = jnp.concatenate([best_ref[:, s * lanes : (s + 1) * lanes] for s in range(len(block))], axis=0)
        summed = group_sum(both, qlen)
        for s in range(len(block)):
            out_ref[start + s : start + s + 1, :] = jnp.sum(
                jnp.where(row == column, summed[s * total : (s + 1) * total], 0.0), axis=0, keepdims=True
            )
        start += 2


def score(query_list, near, far, qlen):
    lanes = query_list[0].shape[1]
    sources = sum(q.shape[0] for q in query_list)
    total = near.shape[0] + far.shape[0]
    return pl.pallas_call(
        functools.partial(score_kernel, qlen, len(query_list)),
        out_shape=jax.ShapeDtypeStruct((sources, lanes), jnp.float32),
        in_specs=[VMEM] * (len(query_list) + 2),
        out_specs=VMEM,
        scratch_shapes=[pltpu.VMEM((total, 2 * lanes), jnp.float32)],
        compiler_params=pltpu.CompilerParams(vmem_limit_bytes=LIMIT),
        cost_estimate=pl.CostEstimate(
            flops=2 * sources * lanes * near.shape[2] * total * near.shape[1],
            bytes_accessed=2 * (near.size + far.size),
            transcendentals=0,
        ),
    )(*query_list, near, far)


def contrast_kernel(
    qlen, query_ref, own_ref, other_ref, where_ref, lane_ref, contrast_ref, index_ref, best_ref, ints_ref
):
    queries = unit(query_ref[...])
    lanes = queries.shape[0]
    docs = own_ref.shape[0]
    total = docs + other_ref.shape[0]
    for i in range(total):
        tokens = own_ref[i] if i < docs else other_ref[i - docs]
        best_ref[i : i + 1, :] = best_match(tokens, queries)
    count, width = where_ref.shape
    index_ref[0:1, :] = flat_lanes(where_ref[...], ints_ref.at[0], lanes)
    lane = flat_lanes(lane_ref[...], ints_ref.at[1], lanes)
    index_ref[1:2, :] = lane + lax.broadcasted_iota(jnp.int32, (1, lanes), 1) // width * (lanes // count)
    logits = group_sum(best_ref[...], qlen)
    row = lax.broadcasted_iota(jnp.int32, (total, lanes), 0)
    query = lax.broadcasted_iota(jnp.int32, (total, lanes), 1) // qlen
    own = jnp.sum(jnp.where(row == query, logits, 0.0), axis=0, keepdims=True)
    loss = jnp.log(jnp.sum(jnp.exp(logits), axis=0, keepdims=True)) - own
    place = (lax.broadcasted_iota(jnp.int32, (8, lanes), 1) * qlen) % lanes
    spread = jnp.take_along_axis(jnp.broadcast_to(loss, (8, lanes)), place, axis=1)
    contrast_ref[...] = spread[0:1, : lanes // qlen]


def contrast_loss(query_rows, own, other, whose, lane, qlen):
    lanes = query_rows.shape[0]
    total = own.shape[0] + other.shape[0]
    return pl.pallas_call(
        functools.partial(contrast_kernel, qlen),
        out_shape=(
            jax.ShapeDtypeStruct((1, lanes // qlen), jnp.float32),
            jax.ShapeDtypeStruct((2, lanes), jnp.int32),
        ),
        in_specs=[VMEM] * 5,
        out_specs=(VMEM, VMEM),
        scratch_shapes=[pltpu.VMEM((total, lanes), jnp.float32), pltpu.VMEM((2, 8, lanes), jnp.int32)],
        compiler_params=pltpu.CompilerParams(vmem_limit_bytes=LIMIT),
        cost_estimate=pl.CostEstimate(
            flops=2 * lanes * own.shape[2] * total * own.shape[1], bytes_accessed=4 * own.size, transcendentals=0
        ),
    )(query_rows, own, other, whose, lane)


def distill_kernel(mine_ref, back_ref, teach_ref, index_ref, student_ref, distill_ref):
    queries, width = student_ref.shape[1:]
    scorers, lanes = 1 + back_ref.shape[0], back_ref.shape[1]
    returned = jnp.concatenate([mine_ref[0:1, :], back_ref[...]], axis=0)
    picked = jnp.take_along_axis(
        returned, jnp.broadcast_to(index_ref[1:2, :], (scorers, lanes)), axis=1
    )
    row = lax.broadcasted_iota(jnp.int32, (scorers, lanes), 0)
    student = jnp.sum(jnp.where(row == index_ref[0:1, :], picked, 0.0), axis=0, keepdims=True)
    first = lax.broadcasted_iota(jnp.int32, (8, lanes), 0)
    place = lax.broadcasted_iota(jnp.int32, (8, lanes), 1)
    spread = jnp.take_along_axis(jnp.broadcast_to(student, (8, lanes)), (first * width + place) % lanes, axis=1)
    student_ref[0] = spread[:queries, :width]
    share = teach_ref[0:1, :]
    sums = group_sum(jnp.concatenate([jnp.exp(student), share * student], axis=0), width, packed=True)
    loss = teach_ref[1:2, :] - sums[1:2] + teach_ref[2:3, :] * jnp.log(sums[0:1])
    distill_ref[...] = loss[:, :queries]


def distill_loss(returned, teach, index, shape):
    return pl.pallas_call(
        distill_kernel,
        out_shape=(
            jax.ShapeDtypeStruct(shape, jnp.float32),
            jax.ShapeDtypeStruct(shape[:2], jnp.float32),
        ),
        in_specs=[VMEM] * 4,
        out_specs=(VMEM, VMEM),
        compiler_params=pltpu.CompilerParams(vmem_limit_bytes=LIMIT),
    )(*returned, teach, index)


def swap(values, axis, bit):
    return lax.ppermute(values, axis, [(i, i ^ bit) for i in range(lax.axis_size(axis))])


def per_device(
    queries, passages, passage_lengths, positives, positive_lengths, owners, local_ids, teacher
):
    peers = lax.axis_size("dp")
    groups = lax.axis_size("blk")
    me = lax.axis_index("dp")
    query_count, qlen = queries.shape[1:3]
    pass_count = passages.shape[1]
    own_rows = queries.reshape(1, query_count * qlen, queries.shape[3])
    bits = [(1 << n) | 1 for n in range(1, peers.bit_length() - 1)]

    tie = lax.optimization_barrier

    last = bits[0]
    near = prepare(passages[0], passage_lengths)
    got = swap(own_rows, "dp", bits[-1])
    positives, got = tie((positives, got))
    far = swap(near, "dp", 1)
    own_docs, teach = prepare_docs(positives[0], positive_lengths, teacher, query_count * qlen)
    parts = [got]
    held = jnp.concatenate([own_rows, got], axis=0)
    crossed = []
    for n, bit in enumerate(reversed(bits[1:-1])):
        got = swap(held, "dp", bit)
        crossing = held if n == 0 else parts[-1]
        if n == 0:
            crossing, own_docs = tie((crossing, own_docs))
        crossed.append(swap(crossing, "dp", last))
        if n == 0:
            got, own_docs, teach = tie((got, own_docs, teach))
        parts.append(got)
        held = jnp.concatenate([held, got], axis=0)
    other_docs = jnp.concatenate(
        [
            lax.ppermute(own_docs, "blk", [(i, (i + k) % groups) for i in range(groups)])
            for k in range(1, groups)
        ],
        axis=0,
    )
    early_cross = score(crossed, near, far, qlen)
    late_cross = swap(parts[-1], "dp", last)
    late_cross, early_cross = tie((late_cross, early_cross))
    late_cross = score([late_cross], near, far, qlen)

    gate = jnp.concatenate([early_cross, late_cross], axis=0)
    arrived = swap(gate[None], "dp", last)
    back = arrived
    for n, bit in enumerate(bits[1:]):
        half = back.shape[1] // 2
        rows = [parts[-1 - n]] if n < len(bits) - 2 else [own_rows, parts[0]]
        rows, gate = tie((rows, gate))
        mine = score(rows, near, far, qlen)
        arrived, mine = tie((arrived, mine))
        if n == 0:
            back = arrived
        gate = arrived
        leaving = jnp.concatenate([mine[None, -half:], back[:, half:]], axis=0)
        if n == len(bits) - 2:
            leaving, other_docs, owners = tie((leaving, other_docs, owners))
            apart = owners[0, :, :, 0] ^ me
            odd = functools.reduce(lambda x, m: x ^ (apart >> m), range(1, peers.bit_length() - 1), apart) & 1
            lane = odd * pass_count + local_ids[0]
            contrast, index = contrast_loss(own_rows[0], own_docs, other_docs, apart >> 1, lane, qlen)
        arrived = swap(leaving, "dp", bit)
        if n == len(bits) - 2:
            arrived, contrast, index = tie((arrived, contrast, index))
        back = jnp.concatenate([back[:, :half], arrived], axis=0)
    returned = [mine, back[:, 0]]
    student, distill = distill_loss(returned, teach, index, teacher.shape)
    return (student, distill, contrast)


def solution(mesh):
    in_specs = (
        P("blk", "dp", None, None),
        P("blk", "dp", None, None),
        P("blk", "dp"),
        P("blk", "dp", None, None),
        P("blk", "dp"),
        P("blk", "dp", None, None),
        P("blk", "dp", None),
        P("blk", "dp", None),
    )
    out_specs = (P("blk", "dp", None), P("blk", "dp"), P("blk", "dp"))
    return jax.shard_map(
        per_device, mesh=mesh, in_specs=in_specs, out_specs=out_specs, check_vma=False
    )
```
